256 devices in a mesh: rep: 32 (over y_lo, z, core), tm: 4 (over x), space: 2 (over y_hi).
Axes of the slice: x: 4, y: 4 (y_hi: 2, y_lo: 2; y = y_hi * 2 + y_lo), z: 8, core: 2. Of those that a mesh axis runs over, the one named last changes fastest.
Arguments:
- spins: float32 [160, 3, 64, 4096], P('rep', None, 'tm', 'space'), may hold values from -4 to 4
- bond_right: float32 [4096], P('space'), may hold values from -4 to 4
- bond_down: float32 [4096], P('space'), may hold values from -4 to 4
- betas: float32 [160], P('rep'), may hold values from 0.2 to 2
- time_coupling: float32 [160], P('rep'), may hold values from 0.1 to 1
- thresholds: int32 [2, 160, 64, 4096], P(None, 'rep', 'tm', 'space'), may hold values from 0 to 8191
- partner: int32 [160], P('rep'), may hold values from 0 to 159, as said below
- accept: int32 [160], P('rep'), may hold values from 0 to 1, as said below
Outputs:
- swapped: float32 [160, 3, 64, 4096], P('rep', None, 'tm', 'space')
- energies: float32 [160, 64], P('rep', 'tm')
The draws below stay inside these ranges and needn't reach their ends.
Inputs may be any that keep to these rules, and one draw needn't show every extreme that they name: partner[r] is r - 1, r or r + 1, and partner[partner[r]] = r; partner[r] = r + 1 wherever r % 5 = 4 and r + 1 < 160. accept[r] = accept[partner[r]], accept[r] = 0 where partner[r] = r, and accept[r] = 1 wherever r % 5 = 4 and r + 1 < 160.
All inputs are finite; a program needn't handle non-finite values.
Results may differ from the reference program's by a relative error of at most 0.0001.
Values sent between devices are 32-bit elements; how exact they have to be, the bound alone decides.
No kernel may reach another device: no remote copies, remote signals or barrier semaphores. Data moves between devices by JAX's collectives and lax.ppermute only.
A program may use at most 64 MiB of HBM per device.

```python
import math
import jax
import jax.numpy as jnp
from jax import lax

REP_DEV = 5
LY = 64
TAU = 64
SITES = 4096
REPS = 160


def pairing(key):
    pick_key = jax.random.fold_in(key, 21)
    flag_key = jax.random.fold_in(key, 22)
    index = jnp.arange(REPS, dtype=jnp.int32)
    place = index % REP_DEV
    boundary = (place == REP_DEV - 1) & (index + 1 < REPS)
    inner = (place >= 1) & (place <= REP_DEV - 3)
    coins = jax.random.randint(pick_key, (REPS,), 0, 2, dtype=jnp.int32)
    wanted = inner & (coins == 1)
    wanted_before = jnp.concatenate([jnp.zeros((1,), dtype=bool), wanted[:-1]])
    chosen = boundary | wanted & jnp.logical_not(wanted_before)
    chosen_before = jnp.concatenate([jnp.zeros((1,), dtype=bool), chosen[:-1]])
    flags = jax.random.randint(flag_key, (REPS,), 0, 4, dtype=jnp.int32)
    edge_accept = jnp.where(boundary, 1, jnp.where(flags >= 1, 1, 0)).astype(jnp.int32)
    accept_before = jnp.concatenate([jnp.zeros((1,), dtype=jnp.int32), edge_accept[:-1]])
    partner = jnp.where(chosen, index + 1, jnp.where(chosen_before, index - 1, index))
    accept = jnp.where(chosen, edge_accept, jnp.where(chosen_before, accept_before, 0))
    return (partner.astype(jnp.int32), accept.astype(jnp.int32))


def draw_partner(key, part):
    return pairing(key)[0]


def draw_accept(key, part):
    return pairing(key)[1]


def plant(array, stream_key, least, high):
    shape = array.shape
    spot = [jax.random.randint(jax.random.fold_in(stream_key, axis), (), 0, shape[axis]) for axis in range(len(shape))]
    array = array.at[tuple(spot)].set(least)
    longest = shape.index(max(shape))
    spot[longest] = (spot[longest] + 1) % shape[longest]
    return array.at[tuple(spot)].set(high)


def block_levels(key, extent, shards, smallest, largest):
    factor_of, own = 1.0, jax.random.fold_in(key, 6)
    for dim, shards_of in shards:
        heights = jnp.exp(jax.random.uniform(jax.random.fold_in(own, dim), (shards_of,), jnp.float32, smallest / len(shards), largest / len(shards)))
        factor_of = factor_of * jnp.repeat(heights, extent[dim] // shards_of).reshape([-1 if axis == dim else 1 for axis in range(len(extent))])
    return factor_of


def centred(rng, extent, spread, reach, cuts=(), kind=jnp.bfloat16):
    values = spread * jax.random.normal(rng, extent, jnp.float32)
    if cuts:
        values = values * block_levels(rng, extent, cuts, -0.22, 0.18)
    return jnp.clip(values, -reach, reach).astype(kind)


def setup_inputs(seed: int = 0) -> dict:
    arg_keys = jax.random.split(jax.random.key(seed), 9)
    spins = centred(arg_keys[0], (REPS, 3, TAU, SITES), 0.6, 4.0, ((0, 32), (2, 4), (3, 2)), jnp.float32)
    bond_right = centred(arg_keys[1], (SITES,), 1.0, 4.0, ((0, 2),), jnp.float32)
    bond_down = centred(arg_keys[2], (SITES,), 1.0, 4.0, ((0, 2),), jnp.float32)
    betas = jnp.clip(jnp.exp(math.log(2.0) - 2.3025851 * jax.random.uniform(arg_keys[3], (REPS,), jnp.float32) ** block_levels(arg_keys[3], (REPS,), ((0, 32),), -0.2, 0.2)), 0.2, 2.0)
    time_coupling = jnp.clip(jnp.exp(math.log(1.0) - 2.3025851 * jax.random.uniform(arg_keys[4], (REPS,), jnp.float32) ** block_levels(arg_keys[4], (REPS,), ((0, 32),), -0.2, 0.2)), 0.1, 1.0)
    thresholds = plant(jax.random.randint(arg_keys[5], (2, REPS, TAU, SITES), 0, 8192), jax.random.fold_in(arg_keys[5], 1), 0, 8191).astype(jnp.int32)
    partner = draw_partner(jax.random.fold_in(arg_keys[8], 71), 0)
    accept = draw_accept(jax.random.fold_in(arg_keys[8], 71), 0)
    return dict(spins=spins, bond_right=bond_right, bond_down=bond_down, betas=betas, time_coupling=time_coupling, thresholds=thresholds, partner=partner, accept=accept)


def reference(spins, bond_right, bond_down, betas, time_coupling, thresholds, partner, accept):
    flat = jnp.arange(SITES)
    column = flat % LY
    row = flat // LY
    level = jnp.arange(TAU)
    parity = (row[None, :] + column[None, :] + level[:, None]) % 2
    bond_up = jnp.roll(bond_down, LY)
    bond_left = jnp.where(column == 0, jnp.roll(bond_right, -(LY - 1)), jnp.roll(bond_right, 1))
    beta_col = betas[:, None, None, None]
    coupling_col = time_coupling[:, None, None, None]
    state = spins
    for half in range(2):
        right = jnp.where(column == LY - 1, jnp.roll(state, LY - 1, axis=3), jnp.roll(state, -1, axis=3))
        left = jnp.where(column == 0, jnp.roll(state, -(LY - 1), axis=3), jnp.roll(state, 1, axis=3))
        down = jnp.roll(state, -LY, axis=3)
        upper = jnp.roll(state, LY, axis=3)
        field_space = bond_down * down + bond_up * upper + bond_right * right + bond_left * left
        later = jnp.roll(state, -1, axis=2)
        earlier = jnp.roll(state, 1, axis=2)
        field = beta_col * field_space + coupling_col * (later + earlier)
        weight = (thresholds[half].astype(jnp.float32) + 0.5) / 8192.0
        moved = state + weight[:, None] * field
        fresh = moved / jnp.sqrt(0.25 + lax.optimization_barrier(jnp.sum(moved * moved, axis=1, keepdims=True)))
        state = jnp.where(parity == half, fresh, state)
    right = jnp.where(column == LY - 1, jnp.roll(state, LY - 1, axis=3), jnp.roll(state, -1, axis=3))
    down = jnp.roll(state, -LY, axis=3)
    bonds = bond_down * lax.optimization_barrier(jnp.sum(state * down, axis=1)) + bond_right * lax.optimization_barrier(jnp.sum(state * right, axis=1))
    energy = -lax.optimization_barrier(jnp.sum(bonds, axis=-1)) / SITES
    source = jnp.where(accept == 1, partner, jnp.arange(REPS).astype(jnp.int32)).astype(jnp.int32)
    return (state[source], energy[source])
```

```python
import jax
import jax.numpy as jnp
from jax import lax
from jax.experimental import pallas as pl
from jax.experimental.pallas import tpu as pltpu
from jax.sharding import PartitionSpec as P

TILES = 16
PLANES = 8
CORE = TILES * PLANES
CORE_MSG = CORE + 2
EDGE = 10
ROWQ = 10
MESSAGE_ROWS = 424
CHUNK = 5
F32 = jnp.float32
VMEM_LIMIT = 48 * 1024 * 1024


def lanes():
    return lax.broadcasted_iota(jnp.int32, (8, 128), 1)


def subs():
    return lax.broadcasted_iota(jnp.int32, (8, 128), 0)


def checker():
    lane = lanes()
    return lax.rem(lane // 64 + lax.rem(lane, 64) + subs(), 2) == 0


def checker_row0(rows):
    lane = lax.broadcasted_iota(jnp.int32, (rows, 128), 1)
    return lax.rem(lane // 64 + lax.rem(lane, 64), 2) == 0


def take(x, index, axis):
    return jnp.take_along_axis(x, index, axis=axis, mode="promise_in_bounds")


def pack_config(spins, thr0, thr1, masks, put):
    mask, flip = masks
    for k in range(TILES):
        for comp in range(3):
            a, b = spins(comp, 0, k), take(spins(comp, 1, k), flip, 0)
            put(comp, k, jnp.where(mask, a, b))
            put(3 + comp, k, jnp.where(mask, b, a))
        a, b = thr0(0, k), take(thr0(1, k), flip, 0)
        put(6, k, (jnp.where(mask, a, b).astype(F32) + 0.5) / 8192.0)
        a, b = thr1(0, k), take(thr1(1, k), flip, 0)
        put(7, k, (jnp.where(mask, b, a).astype(F32) + 0.5) / 8192.0)


def config_reader(spin_buf, thr_buf):
    def spins(comp, half, k):
        return spin_buf[comp, half * 8 : half * 8 + 8, k * 128 : k * 128 + 128]

    def thr(which):
        return lambda half, k: thr_buf[which, half * 8 : half * 8 + 8, k * 128 : k * 128 + 128]

    return spins, thr(0), thr(1)


def edge_message(get, out, base):
    low = lanes() < 64
    last = TILES - 1
    for comp in range(3):
        out[base + comp] = get(3 + comp, 0)
        out[base + 3 + comp] = get(3 + comp, last)
        out[base + 6 + comp] = jnp.where(low, get(comp, 0), get(comp, last))
    out[base + 9] = jnp.where(low, get(6, 0), get(6, last))


def fetch(spins_ref, thr_ref, config, spin_buf, thr_buf, sem, base):
    copies = [
        pltpu.make_async_copy(spins_ref.at[config], spin_buf, sem.at[base]),
        pltpu.make_async_copy(thr_ref.at[0, config], thr_buf.at[0], sem.at[base + 1]),
        pltpu.make_async_copy(thr_ref.at[1, config], thr_buf.at[1], sem.at[base + 2]),
    ]
    for copy in copies:
        copy.start()
    return copies


def far_kernel(spins_ref, thr_ref, beta_ref, coup_ref, core_ref, edge_ref, spin_buf, thr_buf, sem):
    config = jnp.where(lax.rem(lax.axis_index("rep"), 2) == 0, 0, 4)
    copies = fetch(spins_ref, thr_ref, config, spin_buf, thr_buf, sem, 0)
    core_ref[CORE] = jnp.full((8, 128), beta_ref[config], F32)
    core_ref[CORE + 1] = jnp.full((8, 128), coup_ref[config], F32)
    masks = (checker(), 7 - subs())
    for copy in copies:
        copy.wait()

    def put(plane, k, value):
        core_ref[k * PLANES + plane] = value

    pack_config(*config_reader(spin_buf, thr_buf), masks, put)
    edge_message(lambda plane, k: core_ref[k * PLANES + plane], edge_ref, 0)


def near_kernel(
    spins_ref, thr_ref, beta_ref, coup_ref, right_ref, down_ref,
    core_ref, edge_ref, inner_ref, inner_edge_ref, rows_ref,
    spin_buf, thr_buf, sem,
):
    near = jnp.where(lax.rem(lax.axis_index("rep"), 2) == 0, 4, 0)
    copies = [
        fetch(spins_ref, thr_ref, config, spin_buf.at[n], thr_buf.at[n], sem, 3 * n)
        for n, config in enumerate((near, 1, 2, 3))
    ]
    core_ref[CORE] = jnp.full((8, 128), beta_ref[near], F32)
    core_ref[CORE + 1] = jnp.full((8, 128), coup_ref[near], F32)
    last = TILES - 1
    bonds = 3 * EDGE
    inner_edge_ref[bonds] = jnp.zeros((8, 128), F32)
    inner_edge_ref[bonds, 0:1] = down_ref[0:1]
    inner_edge_ref[bonds, 1:2] = down_ref[last : last + 1]
    inner_edge_ref[bonds, 2:3] = right_ref[0:1]
    inner_edge_ref[bonds, 3:4] = right_ref[last : last + 1]
    masks = (checker(), 7 - subs())
    for copy in copies[0]:
        copy.wait()

    def put_core(plane, k, value):
        core_ref[k * PLANES + plane] = value

    pack_config(*config_reader(spin_buf.at[0], thr_buf.at[0]), masks, put_core)
    edge_message(lambda plane, k: core_ref[k * PLANES + plane], edge_ref, 0)
    for n in range(3):
        for copy in copies[n + 1]:
            copy.wait()

        def put(plane, k, value):
            inner_ref[n, k * PLANES + plane] = value
            if plane < 7:
                rows_ref[plane * TILES + k, n : n + 1] = value[0:1]
            if 3 <= plane < 6:
                rows_ref[(plane + 4) * TILES + k, n : n + 1] = value[1:2]

        pack_config(*config_reader(spin_buf.at[n + 1], thr_buf.at[n + 1]), masks, put)
        edge_message(lambda plane, k: inner_ref[n, k * PLANES + plane], inner_edge_ref, n * EDGE)


def slices_kernel(
    rows_ref, x_ref, y_ref, inner_edge_ref, x_edge_ref, y_edge_ref, beta_ref, coup_ref,
    up_ref, down_ref, own_ref,
):
    sub = subs()
    even = checker_row0(8)
    low = lanes() < 64
    swap = jnp.bitwise_xor(lanes(), 1)

    def five(mine, x, y):
        return jnp.where(sub == 3, x, jnp.where(sub == 4, y, mine))

    def row(q, k):
        plane, s = (q, 0) if q < 7 else (q - 4, 1)
        at = k * PLANES + plane
        return five(rows_ref[q * TILES + k], x_ref[at, s : s + 1], y_ref[at, s : s + 1])

    for k in range(TILES):
        p0 = [row(c, k) for c in range(3)]
        p1 = [row(3 + c, k) for c in range(3)]
        w0 = row(6, k)
        second = [row(7 + c, k) for c in range(3)]
        for c in range(3):
            own_ref[k * 3 + c] = p1[c]
        swapped_y, swapped_w = take(second[1], swap, 1), take(w0, swap, 1)
        down = [jnp.where(even, p0[c], p1[c]) for c in range(3)]
        down += [jnp.where(even, second[0], swapped_y), jnp.where(even, second[2], swapped_w)]
        up = [jnp.where(even, p1[c], p0[c]) for c in range(3)]
        up += [jnp.where(even, swapped_y, second[0]), jnp.where(even, swapped_w, second[2])]
        for q in range(CHUNK):
            at = (k * CHUNK + q) * 5
            down_ref[at : at + 5] = down[q][0:5]
            up_ref[at : at + 5] = up[q][0:5]
    for c in range(3):
        merged = []
        for ref, base in ((inner_edge_ref, 0), (inner_edge_ref, EDGE), (inner_edge_ref, 2 * EDGE), (x_edge_ref, 0), (y_edge_ref, 0)):
            merged.append(jnp.where(low[0:1], ref[base + c, 0:1], ref[base + 3 + c, 0:1]))
        corner = five(
            jnp.where(sub == 0, merged[0], jnp.where(sub == 1, merged[1], merged[2])), merged[3], merged[4]
        )
        at = (TILES * CHUNK + c) * 5
        down_ref[at : at + 5] = corner[0:5]
        up_ref[at : at + 5] = corner[0:5]
    at = (TILES * CHUNK + 3) * 5
    down_ref[at:MESSAGE_ROWS] = jnp.zeros((MESSAGE_ROWS - at, 128), F32)
    up_ref[at:MESSAGE_ROWS] = jnp.zeros((MESSAGE_ROWS - at, 128), F32)
    for base, ref in ((0, beta_ref), (1, coup_ref)):
        mine = jnp.where(sub == 0, ref[1], jnp.where(sub == 1, ref[2], ref[3]))
        own_ref[3 * TILES + base] = five(mine, x_ref[CORE + base], y_ref[CORE + base])


def row_neighbours():
    lane = lanes()
    column = lax.rem(lane, 64)
    right = jnp.where(column == 63, lane - 63, lane + 1)
    left = jnp.where(column == 0, lane + 63, lane - 1)
    return right, left


def normalized(moved):
    scale = lax.rsqrt(0.25 + (moved[0] * moved[0] + moved[1] * moved[1] + moved[2] * moved[2]))
    return [m * scale for m in moved]


def sweep_kernel(
    inner_ref, x_ref, y_ref, inner_edge_ref, x_edge_ref, y_edge_ref, own_ref, up_ref, down_ref,
    right_ref, bdown_ref, partner_ref, accept_ref,
    out_ref, energy_ref,
    packed, halo, halo_second, bonds, sem, out_sem, out_buf,
):
    rep = lax.axis_index("rep")
    is_even = lax.rem(rep, 2) == 0
    last = TILES - 1
    sources = [inner_ref.at[0], inner_ref.at[1], inner_ref.at[2], x_ref.at[0:CORE], y_ref.at[0:CORE]]
    copies = [
        pltpu.make_async_copy(source, packed.at[n, PLANES : PLANES + CORE], sem.at[n])
        for n, source in enumerate(sources)
    ]
    for copy in copies:
        copy.start()

    low = lanes() < 64
    sub = subs()
    mask = checker()
    right_at, left_at = row_neighbours()
    flip = 7 - sub

    edge_bonds = 3 * EDGE

    def bond_rows(k):
        if k == -1:
            return inner_edge_ref[edge_bonds, 1:2], inner_edge_ref[edge_bonds, 3:4]
        if k == TILES:
            return inner_edge_ref[edge_bonds, 0:1], inner_edge_ref[edge_bonds, 2:3]
        return bdown_ref[k : k + 1], right_ref[k : k + 1]

    before = jnp.zeros((8, 128), F32)
    for k in range(-1, TILES + 1):
        down, right = (jnp.broadcast_to(row, (8, 128)) for row in bond_rows(k))
        turned = pltpu.roll(down, 64, 1)
        bonds[(k + 1) * 4] = down
        bonds[(k + 1) * 4 + 1] = jnp.where(low, before, turned)
        bonds[(k + 1) * 4 + 2] = right
        bonds[(k + 1) * 4 + 3] = take(right, left_at, 1)
        before = turned

    def space_field(at, above, here, below):
        turned = pltpu.roll(here, 64, 1)
        down = jnp.where(low, turned, below)
        upper = jnp.where(low, above, turned)
        return (
            bonds[at * 4] * down
            + bonds[at * 4 + 1] * upper
            + bonds[at * 4 + 2] * take(here, right_at, 1)
            + bonds[at * 4 + 3] * take(here, left_at, 1)
        )

    even8 = checker_row0(8)
    swap = jnp.bitwise_xor(lanes(), 1)

    def chunk(ref, i):
        at = i * 5
        return ref[at : at + 8]

    beta_rows = own_ref[3 * TILES]
    coup_rows = own_ref[3 * TILES + 1]
    for k in range(TILES):
        for c in range(3):
            up, down = chunk(up_ref, k * CHUNK + c), chunk(down_ref, k * CHUNK + c)
            halo[(k + 1) * 6 + c] = jnp.where(even8, down, up)
            halo[(k + 1) * 6 + 3 + c] = jnp.where(even8, up, down)
    for c in range(3):
        corner = jnp.where(even8, chunk(up_ref, TILES * CHUNK + c), chunk(down_ref, TILES * CHUNK + c))
        halo[3 + c] = corner
        halo[(TILES + 1) * 6 + 3 + c] = corner
    for k in range(TILES):
        a_up, a_down = chunk(up_ref, k * CHUNK + 3), chunk(down_ref, k * CHUNK + 3)
        b_up, b_down = chunk(up_ref, k * CHUNK + 4), chunk(down_ref, k * CHUNK + 4)
        second = [
            jnp.where(even8, a_down, a_up),
            take(jnp.where(even8, a_up, a_down), swap, 1),
            jnp.where(even8, b_down, b_up),
        ]
        weight = take(jnp.where(even8, b_up, b_down), swap, 1)
        moved = []
        for c in range(3):
            above = pltpu.roll(halo[k * 6 + 3 + c], 64, 1)
            below = pltpu.roll(halo[(k + 2) * 6 + 3 + c], 64, 1)
            field = beta_rows * space_field(k + 1, above, halo[(k + 1) * 6 + 3 + c], below)
            field = field + coup_rows * (own_ref[k * 3 + c] + second[c])
            moved.append(halo[(k + 1) * 6 + c] + weight * field)
        fresh = normalized(moved)
        for c in range(3):
            halo_second[k * 3 + c] = fresh[c]

    betas = [own_ref[3 * TILES, n : n + 1] for n in range(5)]
    coups = [own_ref[3 * TILES + 1, n : n + 1] for n in range(5)]
    edges = ((inner_edge_ref, 0), (inner_edge_ref, EDGE), (inner_edge_ref, 2 * EDGE), (x_edge_ref, 0), (y_edge_ref, 0))
    lane = lanes()
    energy_ref[...] = jnp.zeros((8, 128), F32)

    def time_sum(here, outer):
        before = jnp.where(sub == 0, outer, pltpu.roll(here, 1, 0))
        after = jnp.where(sub == 7, here, pltpu.roll(here, 7, 0))
        return before + after

    writes = []
    for n in range(5):
        copies[n].wait()
        ref, base = edges[n]
        work = packed.at[n]
        for c in range(3):
            work[c] = ref[base + 6 + c]
            work[(TILES + 1) * PLANES + c] = ref[base + 6 + c]
            work[3 + c] = ref[base + 3 + c]
            work[(TILES + 1) * PLANES + 3 + c] = ref[base + c]
        work[6] = ref[base + 9]
        work[(TILES + 1) * PLANES + 6] = ref[base + 9]
        beta = jnp.broadcast_to(betas[n], (8, 128))
        coup = jnp.broadcast_to(coups[n], (8, 128))

        def update(p, at, above_at, below_at, outer):
            mine, other = (0, 3) if p == 0 else (3, 0)
            weight = work[at * PLANES + 6 + p]
            fields, moved = [], []
            for c in range(3):
                here = work[at * PLANES + other + c]
                above = pltpu.roll(work[above_at * PLANES + other + c], 64, 1)
                below = pltpu.roll(work[below_at * PLANES + other + c], 64, 1)
                space = space_field(at, above, here, below)
                field = beta * space + coup * time_sum(here, outer(c))
                moved.append(work[at * PLANES + mine + c] + weight * field)
                fields.append(space)
            fresh = normalized(moved)
            for c in range(3):
                work[at * PLANES + mine + c] = fresh[c]
            return fields, fresh

        for at in range(TILES + 2):
            update(
                0, at, max(at - 1, 0), min(at + 1, TILES + 1),
                lambda c: halo[at * 6 + 3 + c, n : n + 1],
            )
        total = jnp.zeros((8, 128), F32)
        for k in range(TILES):
            at = k + 1
            fields, fresh = update(1, at, at - 1, at + 1, lambda c: halo_second[k * 3 + c, n : n + 1])
            total = total + (fresh[0] * fields[0] + fresh[1] * fields[1] + fresh[2] * fields[2])
            for c in range(3):
                p0 = work[at * PLANES + c]
                out_buf[n, c, 0:8, k * 128 : k * 128 + 128] = jnp.where(mask, p0, fresh[c])
                out_buf[n, c, 8:16, k * 128 : k * 128 + 128] = take(jnp.where(mask, fresh[c], p0), flip, 0)
        if n < 3:
            slot = n + 1
        elif n == 3:
            slot = jnp.where(is_even, 4, 0)
        else:
            slot = jnp.where(is_even, 0, 4)
        target = jnp.where(accept_ref[slot] == 1, jnp.clip(partner_ref[slot] - 5 * rep, 0, 4), slot)
        write = pltpu.make_async_copy(out_buf.at[n], out_ref.at[target], out_sem.at[n])
        write.start()
        writes.append(write)
        first = jnp.sum(jnp.where(mask, 0.0, total), axis=1, keepdims=True)
        back = jnp.sum(jnp.where(mask, total, 0.0), axis=1, keepdims=True)
        line = jnp.where(lane == sub, first, 0.0) + jnp.where(lane == 15 - sub, back, 0.0)
        line = jnp.sum(line, axis=0, keepdims=True)
        energy_ref[...] = jnp.where(sub == target, -line / 4096.0, energy_ref[...])
    for write in writes:
        write.wait()


def params():
    return pltpu.CompilerParams(vmem_limit_bytes=VMEM_LIMIT)


def vmem():
    return pl.BlockSpec(memory_space=pltpu.VMEM)


def smem():
    return pl.BlockSpec(memory_space=pltpu.SMEM)


def hbm():
    return pl.BlockSpec(memory_space=pl.ANY)


def shape(*dims):
    return jax.ShapeDtypeStruct(dims, F32)


def on_device(spins, bond_right, bond_down, betas, time_coupling, thresholds, partner, accept):
    ranks, depth = lax.axis_size("rep"), lax.axis_size("tm")
    axes = ("rep", "tm", "space")
    right, down = bond_right.reshape(TILES, 128), bond_down.reshape(TILES, 128)

    def far_of(r):
        other = r - 1 if r % 2 == 0 else r + 1
        return other if 0 <= other < ranks else r

    def near_of(r):
        return r + 1 if r % 2 == 0 else r - 1

    def crosswise(x, of):
        pairs = [
            ((r * depth + t) * 2 + s, (of(r) * depth + t) * 2 + 1 - s)
            for r in range(ranks) for t in range(depth) for s in range(2)
        ]
        return lax.ppermute(x, axes, pairs)

    far_core, far_edge = pl.pallas_call(
        far_kernel,
        out_shape=(shape(CORE_MSG, 8, 128), shape(EDGE, 8, 128)),
        in_specs=[hbm(), hbm(), smem(), smem()],
        out_specs=(vmem(), vmem()),
        scratch_shapes=[
            pltpu.VMEM((3, 16, 2048), F32),
            pltpu.VMEM((2, 16, 2048), jnp.int32),
            pltpu.SemaphoreType.DMA((3,)),
        ],
        compiler_params=params(),
        name="pack_far",
    )(spins, thresholds, betas, time_coupling)
    far_core = lax.ppermute(far_core, "rep", [(r, far_of(r)) for r in range(ranks)])
    far_edge = crosswise(far_edge, far_of)

    near_core, near_edge, inner, inner_edge, rows = pl.pallas_call(
        near_kernel,
        out_shape=(
            shape(CORE_MSG, 8, 128), shape(EDGE, 8, 128), shape(3, CORE, 8, 128),
            shape(3 * EDGE + 1, 8, 128), shape(ROWQ * TILES, 8, 128),
        ),
        in_specs=[hbm(), hbm(), smem(), smem(), vmem(), vmem()],
        out_specs=(vmem(),) * 5,
        scratch_shapes=[
            pltpu.VMEM((4, 3, 16, 2048), F32),
            pltpu.VMEM((4, 2, 16, 2048), jnp.int32),
            pltpu.SemaphoreType.DMA((12,)),
        ],
        compiler_params=params(),
        name="pack_near",
    )(spins, thresholds, betas, time_coupling, right, down)
    near_core = lax.ppermute(near_core, "rep", [(r, near_of(r)) for r in range(ranks)])
    near_edge = crosswise(near_edge, near_of)
    inner_edge = lax.ppermute(inner_edge, "space", [(0, 1), (1, 0)])

    message = shape(MESSAGE_ROWS, 128)
    up, down_msg, own = pl.pallas_call(
        slices_kernel,
        out_shape=(message, message, shape(3 * TILES + 2, 8, 128)),
        in_specs=[vmem()] * 6 + [smem()] * 2,
        out_specs=(vmem(),) * 3,
        compiler_params=params(),
        name="slices",
    )(rows, near_core, far_core, inner_edge, near_edge, far_edge, betas, time_coupling)
    from_before = lax.ppermute(up, "tm", [(t, (t + 1) % depth) for t in range(depth)])
    from_after = lax.ppermute(down_msg, "tm", [((t + 1) % depth, t) for t in range(depth)])

    swapped, energy = pl.pallas_call(
        sweep_kernel,
        out_shape=(shape(5, 3, 16, 2048), shape(8, 128)),
        in_specs=[hbm()] * 3 + [vmem()] * 8 + [smem()] * 2,
        out_specs=(hbm(), vmem()),
        scratch_shapes=[
            pltpu.VMEM((5, (TILES + 2) * PLANES, 8, 128), F32),
            pltpu.VMEM(((TILES + 2) * 6, 8, 128), F32),
            pltpu.VMEM((TILES * 3, 8, 128), F32),
            pltpu.VMEM(((TILES + 2) * 4, 8, 128), F32),
            pltpu.SemaphoreType.DMA((5,)),
            pltpu.SemaphoreType.DMA((5,)),
            pltpu.VMEM((5, 3, 16, 2048), F32),
        ],
        compiler_params=params(),
        name="sweep",
    )(
        inner, near_core, far_core, inner_edge, near_edge, far_edge, own, from_before, from_after,
        right, down, partner, accept,
    )
    energy = energy + lax.ppermute(energy, "space", [(0, 1), (1, 0)])
    return swapped, energy[:5, :16]


def solution(mesh):
    placed = (
        P("rep", None, "tm", "space"),
        P("space"),
        P("space"),
        P("rep"),
        P("rep"),
        P(None, "rep", "tm", "space"),
        P("rep"),
        P("rep"),
    )
    return jax.shard_map(
        on_device,
        mesh=mesh,
        in_specs=placed,
        out_specs=(P("rep", None, "tm", "space"), P("rep", "tm")),
        check_vma=False,
    )
```

```python
import jax
import jax.numpy as jnp
from jax import lax
from jax.experimental import pallas as pl
from jax.experimental.pallas import tpu as pltpu
from jax.sharding import PartitionSpec as P

TILES = 16
PLANES = 8
CORE = TILES * PLANES
CORE_MSG = CORE + 2
EDGE = 10
ROWQ = 10
MESSAGE_ROWS = 424
CHUNK = 5
F32 = jnp.float32
VMEM_LIMIT = 16 * 1024 * 1024
FRONT_LIMIT = 61 * 1024 * 1024
INNER_LIMIT = 16 * 1024 * 1024


def lanes():
    return lax.broadcasted_iota(jnp.int32, (8, 128), 1)


def subs():
    return lax.broadcasted_iota(jnp.int32, (8, 128), 0)


def checker():
    lane = lanes()
    return lax.rem(lane // 64 + lax.rem(lane, 64) + subs(), 2) == 0


def checker_row0(rows):
    lane = lax.broadcasted_iota(jnp.int32, (rows, 128), 1)
    return lax.rem(lane // 64 + lax.rem(lane, 64), 2) == 0


def take(x, index, axis):
    return jnp.take_along_axis(x, index, axis=axis, mode="promise_in_bounds")


def pack_config(spins, thr0, thr1, masks, put):
    mask, flip = masks
    for k in range(TILES):
        for comp in range(3):
            a, b = spins(comp, 0, k), take(spins(comp, 1, k), flip, 0)
            put(comp, k, jnp.where(mask, a, b))
            put(3 + comp, k, jnp.where(mask, b, a))
        a, b = thr0(0, k), take(thr0(1, k), flip, 0)
        put(6, k, (jnp.where(mask, a, b).astype(F32) + 0.5) / 8192.0)
        a, b = thr1(0, k), take(thr1(1, k), flip, 0)
        put(7, k, (jnp.where(mask, b, a).astype(F32) + 0.5) / 8192.0)


def config_reader(spin_buf, thr_buf):
    def spins(comp, half, k):
        return spin_buf[comp, half * 8 : half * 8 + 8, k * 128 : k * 128 + 128]

    def thr(which):
        return lambda half, k: thr_buf[which, half * 8 : half * 8 + 8, k * 128 : k * 128 + 128]

    return spins, thr(0), thr(1)


def edge_message(spins, thr, masks, out, base):
    mask, flip = masks
    low = lanes() < 64
    for comp in range(3):
        own = []
        for side in range(2):
            a, b = spins(side, comp, 0), take(spins(side, comp, 1), flip, 0)
            own.append(jnp.where(mask, a, b))
            out[base + 3 * side + comp] = jnp.where(mask, b, a)
        out[base + 6 + comp] = jnp.where(low, own[0], own[1])
    steps = [jnp.where(mask, thr(side, 0), take(thr(side, 1), flip, 0)) for side in range(2)]
    out[base + 9] = (jnp.where(low, steps[0], steps[1]).astype(F32) + 0.5) / 8192.0


def fetch(spins_ref, thr_ref, config, spin_buf, thr_buf, sem, base):
    copies = [
        pltpu.make_async_copy(spins_ref.at[config], spin_buf, sem.at[base]),
        pltpu.make_async_copy(thr_ref.at[0, config], thr_buf.at[0], sem.at[base + 1]),
        pltpu.make_async_copy(thr_ref.at[1, config], thr_buf.at[1], sem.at[base + 2]),
    ]
    for copy in copies:
        copy.start()
    return copies


def scalars(beta_ref, coup_ref, beta_buf, coup_buf, sem, base):
    copies = [
        pltpu.make_async_copy(beta_ref, beta_buf, sem.at[base]),
        pltpu.make_async_copy(coup_ref, coup_buf, sem.at[base + 1]),
    ]
    for copy in copies:
        copy.start()
    return copies


def front_kernel(
    spins_ref, thr_ref, beta_ref, coup_ref, right_ref, down_ref,
    far_ref, near_ref, far_edge_ref, near_edge_ref, inner_edge_ref,
    edge_spins, edge_thr, spin_buf, thr_buf, right_buf, down_buf, beta_buf, coup_buf, sem,
):
    is_even = lax.rem(lax.axis_index("rep"), 2) == 0
    far, near = jnp.where(is_even, 0, 4), jnp.where(is_even, 4, 0)
    last = TILES - 1
    edge_copies = []
    for side in range(2):
        at = pl.ds(side * last * 128, 128)
        edge_copies.append(
            pltpu.make_async_copy(spins_ref.at[:, :, :, at], edge_spins.at[side], sem.at[side])
        )
        edge_copies.append(
            pltpu.make_async_copy(thr_ref.at[0, :, :, at], edge_thr.at[side], sem.at[2 + side])
        )
    edge_copies.append(pltpu.make_async_copy(right_ref, right_buf, sem.at[4]))
    edge_copies.append(pltpu.make_async_copy(down_ref, down_buf, sem.at[5]))
    for copy in edge_copies:
        copy.start()
    small = scalars(beta_ref, coup_ref, beta_buf, coup_buf, sem, 6)
    leaving = [
        fetch(spins_ref, thr_ref, config, spin_buf.at[n], thr_buf.at[n], sem, 8 + 3 * n)
        for n, config in enumerate((far, near))
    ]
    masks = (checker(), 7 - subs())
    for copy in edge_copies:
        copy.wait()
    bonds = 3 * EDGE
    inner_edge_ref[bonds] = jnp.zeros((8, 128), F32)
    inner_edge_ref[bonds, 0:1] = down_buf[0:1]
    inner_edge_ref[bonds, 1:2] = down_buf[last : last + 1]
    inner_edge_ref[bonds, 2:3] = right_buf[0:1]
    inner_edge_ref[bonds, 3:4] = right_buf[last : last + 1]
    for config, out, base in (
        (1, inner_edge_ref, 0), (2, inner_edge_ref, EDGE), (3, inner_edge_ref, 2 * EDGE),
        (near, near_edge_ref, 0), (far, far_edge_ref, 0),
    ):
        edge_message(
            lambda side, comp, half: edge_spins[side, config, comp, half * 8 : half * 8 + 8],
            lambda side, half: edge_thr[side, config, half * 8 : half * 8 + 8],
            masks, out, base,
        )
    for copy in small:
        copy.wait()
    for n, (config, out) in enumerate(((far, far_ref), (near, near_ref))):
        out[CORE] = jnp.full((8, 128), beta_buf[config], F32)
        out[CORE + 1] = jnp.full((8, 128), coup_buf[config], F32)
        for copy in leaving[n]:
            copy.wait()

        def put(plane, k, value):
            out[k * PLANES + plane] = value

        pack_config(*config_reader(spin_buf.at[n], thr_buf.at[n]), masks, put)


def inner_kernel(
    spins_ref, thr_ref, beta_ref, coup_ref,
    inner_ref, rows_ref, scale_ref,
    spin_buf, thr_buf, beta_buf, coup_buf, sem,
):
    copies = [
        fetch(spins_ref, thr_ref, n + 1, spin_buf.at[n], thr_buf.at[n], sem, 3 * n) for n in range(3)
    ]
    small = scalars(beta_ref, coup_ref, beta_buf, coup_buf, sem, 9)
    masks = (checker(), 7 - subs())
    for n in range(3):
        for copy in copies[n]:
            copy.wait()

        def put(plane, k, value):
            inner_ref[n, k * PLANES + plane] = value
            if plane < 7:
                rows_ref[plane * TILES + k, n : n + 1] = value[0:1]
            if 3 <= plane < 6:
                rows_ref[(plane + 4) * TILES + k, n : n + 1] = value[1:2]

        pack_config(*config_reader(spin_buf.at[n], thr_buf.at[n]), masks, put)
    for copy in small:
        copy.wait()
    sub = subs()
    for base, buf in ((0, beta_buf), (1, coup_buf)):
        scale_ref[base] = jnp.where(sub == 0, buf[1], jnp.where(sub == 1, buf[2], buf[3]))


def slices_kernel(
    rows_ref, scale_ref, x_ref, y_ref, inner_edge_ref, x_edge_ref, y_edge_ref,
    up_ref, down_ref, own_ref,
):
    sub = subs()
    even = checker_row0(8)
    low = lanes() < 64
    swap = jnp.bitwise_xor(lanes(), 1)

    def five(mine, x, y):
        return jnp.where(sub == 3, x, jnp.where(sub == 4, y, mine))

    def row(q, k):
        plane, s = (q, 0) if q < 7 else (q - 4, 1)
        at = k * PLANES + plane
        return five(rows_ref[q * TILES + k], x_ref[at, s : s + 1], y_ref[at, s : s + 1])

    for k in range(TILES):
        p0 = [row(c, k) for c in range(3)]
        p1 = [row(3 + c, k) for c in range(3)]
        w0 = row(6, k)
        second = [row(7 + c, k) for c in range(3)]
        for c in range(3):
            own_ref[k * 3 + c] = p1[c]
        swapped_y, swapped_w = take(second[1], swap, 1), take(w0, swap, 1)
        down = [jnp.where(even, p0[c], p1[c]) for c in range(3)]
        down += [jnp.where(even, second[0], swapped_y), jnp.where(even, second[2], swapped_w)]
        up = [jnp.where(even, p1[c], p0[c]) for c in range(3)]
        up += [jnp.where(even, swapped_y, second[0]), jnp.where(even, swapped_w, second[2])]
        for q in range(CHUNK):
            at = (k * CHUNK + q) * 5
            down_ref[at : at + 5] = down[q][0:5]
            up_ref[at : at + 5] = up[q][0:5]
    for c in range(3):
        merged = []
        for ref, base in ((inner_edge_ref, 0), (inner_edge_ref, EDGE), (inner_edge_ref, 2 * EDGE), (x_edge_ref, 0), (y_edge_ref, 0)):
            merged.append(jnp.where(low[0:1], ref[base + c, 0:1], ref[base + 3 + c, 0:1]))
        corner = five(
            jnp.where(sub == 0, merged[0], jnp.where(sub == 1, merged[1], merged[2])), merged[3], merged[4]
        )
        at = (TILES * CHUNK + c) * 5
        down_ref[at : at + 5] = corner[0:5]
        up_ref[at : at + 5] = corner[0:5]
    at = (TILES * CHUNK + 3) * 5
    down_ref[at:MESSAGE_ROWS] = jnp.zeros((MESSAGE_ROWS - at, 128), F32)
    up_ref[at:MESSAGE_ROWS] = jnp.zeros((MESSAGE_ROWS - at, 128), F32)
    for base in range(2):
        own_ref[3 * TILES + base] = five(scale_ref[base], x_ref[CORE + base], y_ref[CORE + base])


def row_neighbours():
    lane = lanes()
    column = lax.rem(lane, 64)
    right = jnp.where(column == 63, lane - 63, lane + 1)
    left = jnp.where(column == 0, lane + 63, lane - 1)
    return right, left


def normalized(moved):
    scale = lax.rsqrt(0.25 + (moved[0] * moved[0] + moved[1] * moved[1] + moved[2] * moved[2]))
    return [m * scale for m in moved]


def edge_list(inner_edge_ref, x_edge_ref, y_edge_ref):
    inner = [(inner_edge_ref, n * EDGE) for n in range(3)]
    return inner + [(x_edge_ref, 0), (y_edge_ref, 0)]


def core_list(inner_ref, x_ref, y_ref):
    return [inner_ref.at[0], inner_ref.at[1], inner_ref.at[2], x_ref, y_ref]


def space_field(bonds, at, above, here, turned, below, masks):
    low, right_at, left_at = masks
    return (
        bonds[at * 4] * jnp.where(low, turned, below)
        + bonds[at * 4 + 1] * jnp.where(low, above, turned)
        + bonds[at * 4 + 2] * take(here, right_at, 1)
        + bonds[at * 4 + 3] * take(here, left_at, 1)
    )


def turn(x):
    return pltpu.roll(x, 64, 1)


def prepare_kernel(
    inner_ref, x_ref, y_ref, inner_edge_ref, x_edge_ref, y_edge_ref, own_ref, right_ref, bdown_ref,
    moved_ref, bonds,
):
    low = lanes() < 64
    sub = subs()
    right_at, left_at = row_neighbours()
    masks = (low, right_at, left_at)
    edge_bonds = 3 * EDGE

    def bond_rows(k):
        if k == -1:
            return inner_edge_ref[edge_bonds, 1:2], inner_edge_ref[edge_bonds, 3:4]
        if k == TILES:
            return inner_edge_ref[edge_bonds, 0:1], inner_edge_ref[edge_bonds, 2:3]
        return bdown_ref[k : k + 1], right_ref[k : k + 1]

    before = jnp.zeros((8, 128), F32)
    for k in range(-1, TILES + 1):
        down, right = (jnp.broadcast_to(row, (8, 128)) for row in bond_rows(k))
        turned = turn(down)
        bonds[(k + 1) * 4] = down
        bonds[(k + 1) * 4 + 1] = jnp.where(low, before, turned)
        bonds[(k + 1) * 4 + 2] = right
        bonds[(k + 1) * 4 + 3] = take(right, left_at, 1)
        before = turned

    edges = edge_list(inner_edge_ref, x_edge_ref, y_edge_ref)
    for n, core in enumerate(core_list(inner_ref, x_ref, y_ref)):
        edge, base = edges[n]
        beta = jnp.broadcast_to(own_ref[3 * TILES, n : n + 1], (8, 128))
        coup = jnp.broadcast_to(own_ref[3 * TILES + 1, n : n + 1], (8, 128))

        def second(at, c):
            if at == 0:
                return edge[base + 3 + c]
            if at == TILES + 1:
                return edge[base + c]
            return core[(at - 1) * PLANES + 3 + c]

        here = [second(0, c) for c in range(3)]
        turned = [turn(x) for x in here]
        above = turned
        for at in range(TILES + 2):
            outer = at == 0 or at == TILES + 1
            if at <= TILES:
                following = [second(at + 1, c) for c in range(3)]
                below = [turn(x) for x in following]
            else:
                following, below = here, turned
            weight = edge[base + 9] if outer else core[(at - 1) * PLANES + 6]
            for c in range(3):
                x = here[c]
                space = space_field(bonds, at, above[c], x, turned[c], below[c], masks)
                inside = jnp.where(sub == 0, 0.0, pltpu.roll(x, 1, 0)) + jnp.where(sub == 7, x, pltpu.roll(x, 7, 0))
                mine = edge[base + 6 + c] if outer else core[(at - 1) * PLANES + c]
                moved_ref[n, at * 3 + c] = mine + weight * (beta * space + coup * inside)
            above, turned, here = turned, below, following


def sweep_kernel(
    inner_ref, x_ref, y_ref, inner_edge_ref, x_edge_ref, y_edge_ref, own_ref, moved_ref, bonds, up_ref, down_ref,
    partner_ref, accept_ref,
    final_ref, energy_ref,
    halo, halo_first,
):
    rep = lax.axis_index("rep")
    is_even = lax.rem(rep, 2) == 0
    low = lanes() < 64
    sub = subs()
    lane = lanes()
    mask = checker()
    right_at, left_at = row_neighbours()
    masks = (low, right_at, left_at)

    even8 = checker_row0(8)
    swap = jnp.bitwise_xor(lanes(), 1)

    def chunk(ref, i):
        at = i * 5
        return ref[at : at + 8]

    beta_rows = own_ref[3 * TILES]
    coup_rows = own_ref[3 * TILES + 1]
    for k in range(TILES):
        for c in range(3):
            up, down = chunk(up_ref, k * CHUNK + c), chunk(down_ref, k * CHUNK + c)
            halo[(k + 1) * 3 + c] = jnp.where(even8, up, down)
            halo_first[k * 3 + c] = jnp.where(even8, down, up)
    for c in range(3):
        corner = jnp.where(even8, chunk(up_ref, TILES * CHUNK + c), chunk(down_ref, TILES * CHUNK + c))
        halo[c] = corner
        halo[(TILES + 1) * 3 + c] = corner
    here = [halo[3 + c] for c in range(3)]
    above, turned = [turn(halo[c]) for c in range(3)], [turn(x) for x in here]
    for k in range(TILES):
        following = [halo[(k + 2) * 3 + c] for c in range(3)]
        below = [turn(x) for x in following]
        a_up, a_down = chunk(up_ref, k * CHUNK + 3), chunk(down_ref, k * CHUNK + 3)
        b_up, b_down = chunk(up_ref, k * CHUNK + 4), chunk(down_ref, k * CHUNK + 4)
        second = [
            jnp.where(even8, a_down, a_up),
            take(jnp.where(even8, a_up, a_down), swap, 1),
            jnp.where(even8, b_down, b_up),
        ]
        weight = take(jnp.where(even8, b_up, b_down), swap, 1)
        moved = []
        for c in range(3):
            field = beta_rows * space_field(bonds, k + 1, above[c], here[c], turned[c], below[c], masks)
            field = field + coup_rows * (own_ref[k * 3 + c] + second[c])
            moved.append(halo_first[k * 3 + c] + weight * field)
        fresh = normalized(moved)
        for c in range(3):
            halo_first[k * 3 + c] = fresh[c]
        above, turned, here = turned, below, following

    edges = edge_list(inner_edge_ref, x_edge_ref, y_edge_ref)
    energy_ref[...] = jnp.zeros((8, 128), F32)
    for n, core in enumerate(core_list(inner_ref, x_ref, y_ref)):
        edge, base = edges[n]
        beta = jnp.broadcast_to(own_ref[3 * TILES, n : n + 1], (8, 128))
        coup = jnp.broadcast_to(own_ref[3 * TILES + 1, n : n + 1], (8, 128))
        coup_outer = jnp.where(sub == 0, coup, 0.0)
        if n < 3:
            slot = n + 1
        elif n == 3:
            slot = jnp.where(is_even, 4, 0)
        else:
            slot = jnp.where(is_even, 0, 4)
        target = jnp.where(accept_ref[slot] == 1, jnp.clip(partner_ref[slot] - 5 * rep, 0, 4), slot)

        def pass_0(at):
            outer = at == 0 or at == TILES + 1
            factor = (edge[base + 9] if outer else core[(at - 1) * PLANES + 6]) * coup_outer
            fresh = normalized([
                moved_ref[n, at * 3 + c] + factor * halo[at * 3 + c, n : n + 1] for c in range(3)
            ])
            if not outer:
                for c in range(3):
                    final_ref[target, (at - 1) * 6 + c] = fresh[c]
            return fresh, [turn(x) for x in fresh]

        _, above = pass_0(0)
        here, turned = pass_0(1)
        total = jnp.zeros((8, 128), F32)
        for k in range(TILES):
            following, below = pass_0(k + 2)
            weight = core[k * PLANES + 7]
            fields, moved = [], []
            for c in range(3):
                x = here[c]
                space = space_field(bonds, k + 1, above[c], x, turned[c], below[c], masks)
                outside = halo_first[k * 3 + c, n : n + 1]
                around = jnp.where(sub == 0, outside, pltpu.roll(x, 1, 0)) + jnp.where(sub == 7, x, pltpu.roll(x, 7, 0))
                moved.append(core[k * PLANES + 3 + c] + weight * (beta * space + coup * around))
                fields.append(space)
            fresh = normalized(moved)
            total = total + (fresh[0] * fields[0] + fresh[1] * fields[1] + fresh[2] * fields[2])
            for c in range(3):
                final_ref[target, k * 6 + 3 + c] = fresh[c]
            above, turned, here = turned, below, following
        head = jnp.sum(jnp.where(mask, 0.0, total), axis=1, keepdims=True)
        back = jnp.sum(jnp.where(mask, total, 0.0), axis=1, keepdims=True)
        line = jnp.where(lane == sub, head, 0.0) + jnp.where(lane == 15 - sub, back, 0.0)
        line = jnp.sum(line, axis=0, keepdims=True)
        energy_ref[...] = jnp.where(sub == target, -line / 4096.0, energy_ref[...])


def unpack_kernel(final_ref, out_ref, out_buf, sem):
    mask = checker()
    flip = 7 - subs()
    writes = []
    for n in range(5):
        for k in range(TILES):
            for c in range(3):
                p0, p1 = final_ref[n, k * 6 + c], final_ref[n, k * 6 + 3 + c]
                out_buf[n, c, 0:8, k * 128 : k * 128 + 128] = jnp.where(mask, p0, p1)
                out_buf[n, c, 8:16, k * 128 : k * 128 + 128] = take(jnp.where(mask, p1, p0), flip, 0)
        write = pltpu.make_async_copy(out_buf.at[n], out_ref.at[n], sem.at[n])
        write.start()
        writes.append(write)
    for write in writes:
        write.wait()


def params(limit=VMEM_LIMIT):
    return pltpu.CompilerParams(vmem_limit_bytes=limit)


def vmem():
    return pl.BlockSpec(memory_space=pltpu.VMEM)


def smem():
    return pl.BlockSpec(memory_space=pltpu.SMEM)


def hbm():
    return pl.BlockSpec(memory_space=pltpu.HBM)


def anywhere():
    return pl.BlockSpec(memory_space=pl.ANY)


def shape(*dims):
    return jax.ShapeDtypeStruct(dims, F32)


def on_device(spins, bond_right, bond_down, betas, time_coupling, thresholds, partner, accept):
    ranks, depth = lax.axis_size("rep"), lax.axis_size("tm")
    axes = ("rep", "tm", "space")
    right, down = bond_right.reshape(TILES, 128), bond_down.reshape(TILES, 128)

    def far_of(r):
        other = r - 1 if r % 2 == 0 else r + 1
        return other if 0 <= other < ranks else r

    def near_of(r):
        return r + 1 if r % 2 == 0 else r - 1

    def crosswise(x, of):
        pairs = [
            ((r * depth + t) * 2 + s, (of(r) * depth + t) * 2 + 1 - s)
            for r in range(ranks) for t in range(depth) for s in range(2)
        ]
        return lax.ppermute(x, axes, pairs)

    far_core, near_core, far_edge, near_edge, inner_edge = pl.pallas_call(
        front_kernel,
        out_shape=(
            shape(CORE_MSG, 8, 128), shape(CORE_MSG, 8, 128),
            shape(EDGE, 8, 128), shape(EDGE, 8, 128), shape(3 * EDGE + 1, 8, 128),
        ),
        in_specs=[hbm()] * 6,
        out_specs=(vmem(),) * 5,
        scratch_shapes=[
            pltpu.VMEM((2, 5, 3, 16, 128), F32),
            pltpu.VMEM((2, 5, 16, 128), jnp.int32),
            pltpu.VMEM((2, 3, 16, 2048), F32),
            pltpu.VMEM((2, 2, 16, 2048), jnp.int32),
            pltpu.VMEM((TILES, 128), F32),
            pltpu.VMEM((TILES, 128), F32),
            pltpu.SMEM((5,), F32),
            pltpu.SMEM((5,), F32),
            pltpu.SemaphoreType.DMA((14,)),
        ],
        compiler_params=params(FRONT_LIMIT),
        name="front",
    )(spins, thresholds, betas, time_coupling, right, down)
    far_core = lax.ppermute(far_core, "rep", [(r, far_of(r)) for r in range(ranks)])
    inner_edge = lax.ppermute(inner_edge, "space", [(0, 1), (1, 0)])
    far_edge = crosswise(far_edge, far_of)
    near_edge = crosswise(near_edge, near_of)
    near_core = lax.ppermute(near_core, "rep", [(r, near_of(r)) for r in range(ranks)])

    inner, rows, scale = pl.pallas_call(
        inner_kernel,
        out_shape=(shape(3, CORE, 8, 128), shape(ROWQ * TILES, 8, 128), shape(2, 8, 128)),
        in_specs=[hbm()] * 4,
        out_specs=(vmem(),) * 3,
        scratch_shapes=[
            pltpu.VMEM((3, 3, 16, 2048), F32),
            pltpu.VMEM((3, 2, 16, 2048), jnp.int32),
            pltpu.SMEM((5,), F32),
            pltpu.SMEM((5,), F32),
            pltpu.SemaphoreType.DMA((11,)),
        ],
        compiler_params=params(INNER_LIMIT),
        name="pack_inner",
    )(spins, thresholds, betas, time_coupling)

    message = shape(MESSAGE_ROWS, 128)
    up, down_msg, own = pl.pallas_call(
        slices_kernel,
        out_shape=(message, message, shape(3 * TILES + 2, 8, 128)),
        in_specs=[vmem()] * 7,
        out_specs=(vmem(),) * 3,
        compiler_params=params(),
        name="slices",
    )(rows, scale, near_core, far_core, inner_edge, near_edge, far_edge)
    from_before = lax.ppermute(up, "tm", [(t, (t + 1) % depth) for t in range(depth)])
    from_after = lax.ppermute(down_msg, "tm", [((t + 1) % depth, t) for t in range(depth)])

    edges = (inner_edge, near_edge, far_edge)
    moved, bonds = pl.pallas_call(
        prepare_kernel,
        out_shape=(shape(5, (TILES + 2) * 3, 8, 128), shape((TILES + 2) * 4, 8, 128)),
        in_specs=[vmem()] * 9,
        out_specs=(vmem(),) * 2,
        compiler_params=params(),
        name="prepare",
    )(inner, near_core, far_core, *edges, own, right, down)
    final, energy = pl.pallas_call(
        sweep_kernel,
        out_shape=(shape(5, TILES * 6, 8, 128), shape(8, 128)),
        in_specs=[vmem()] * 11 + [smem()] * 2,
        out_specs=(vmem(),) * 2,
        scratch_shapes=[
            pltpu.VMEM(((TILES + 2) * 3, 8, 128), F32),
            pltpu.VMEM((TILES * 3, 8, 128), F32),
        ],
        compiler_params=params(),
        name="sweep",
    )(
        inner, near_core, far_core, *edges, own, moved, bonds, from_before, from_after, partner, accept,
    )
    other_energy = lax.ppermute(energy, "space", [(0, 1), (1, 0)])
    swapped = pl.pallas_call(
        unpack_kernel,
        out_shape=shape(5, 3, 16, 2048),
        in_specs=[vmem()],
        out_specs=hbm(),
        scratch_shapes=[pltpu.VMEM((5, 3, 16, 2048), F32), pltpu.SemaphoreType.DMA((5,))],
        compiler_params=params(),
        name="unpack",
    )(final)
    energy = energy + other_energy
    return swapped, energy[:5, :16]


def solution(mesh):
    placed = (
        P("rep", None, "tm", "space"),
        P("space"),
        P("space"),
        P("rep"),
        P("rep"),
        P(None, "rep", "tm", "space"),
        P("rep"),
        P("rep"),
    )
    return jax.shard_map(
        on_device,
        mesh=mesh,
        in_specs=placed,
        out_specs=(P("rep", None, "tm", "space"), P("rep", "tm")),
        check_vma=False,
    )
```

```python
import jax
import jax.numpy as jnp
from jax import lax
from jax.experimental import pallas as pl
from jax.experimental.pallas import tpu as pltpu
from jax.sharding import PartitionSpec as P

TILES = 16
PLANES = 8
CORE = TILES * PLANES
CORE_MSG = CORE + 2
EDGE = 10
FAR_EDGE = EDGE + 1
ROWQ = 10
MESSAGE_ROWS = 424
CHUNK = 5
F32 = jnp.float32
VMEM_LIMIT = 16 * 1024 * 1024
FRONT_LIMIT = 61 * 1024 * 1024
INNER_LIMIT = 16 * 1024 * 1024


def lanes():
    return lax.broadcasted_iota(jnp.int32, (8, 128), 1)


def subs():
    return lax.broadcasted_iota(jnp.int32, (8, 128), 0)


def checker():
    lane = lanes()
    return lax.rem(lane // 64 + lax.rem(lane, 64) + subs(), 2) == 0


def checker_row0(rows):
    lane = lax.broadcasted_iota(jnp.int32, (rows, 128), 1)
    return lax.rem(lane // 64 + lax.rem(lane, 64), 2) == 0


def take(x, index, axis):
    return jnp.take_along_axis(x, index, axis=axis, mode="promise_in_bounds")


def pack_config(spins, thr0, thr1, masks, put):
    mask, flip = masks
    for k in range(TILES):
        for comp in range(3):
            a, b = spins(comp, 0, k), take(spins(comp, 1, k), flip, 0)
            put(comp, k, jnp.where(mask, a, b))
            put(3 + comp, k, jnp.where(mask, b, a))
        a, b = thr0(0, k), take(thr0(1, k), flip, 0)
        put(6, k, (jnp.where(mask, a, b).astype(F32) + 0.5) / 8192.0)
        a, b = thr1(0, k), take(thr1(1, k), flip, 0)
        put(7, k, (jnp.where(mask, b, a).astype(F32) + 0.5) / 8192.0)


def config_reader(spin_buf, thr_buf):
    def spins(comp, half, k):
        return spin_buf[comp, half * 8 : half * 8 + 8, k * 128 : k * 128 + 128]

    def thr(which):
        return lambda half, k: thr_buf[which, half * 8 : half * 8 + 8, k * 128 : k * 128 + 128]

    return spins, thr(0), thr(1)


def edge_message(spins, thr, masks, out, base):
    mask, flip = masks
    low = lanes() < 64
    for comp in range(3):
        own = []
        for side in range(2):
            a, b = spins(side, comp, 0), take(spins(side, comp, 1), flip, 0)
            own.append(jnp.where(mask, a, b))
            out[base + 3 * side + comp] = jnp.where(mask, b, a)
        out[base + 6 + comp] = jnp.where(low, own[0], own[1])
    steps = [jnp.where(mask, thr(side, 0), take(thr(side, 1), flip, 0)) for side in range(2)]
    out[base + 9] = (jnp.where(low, steps[0], steps[1]).astype(F32) + 0.5) / 8192.0


def fetch(spins_ref, thr_ref, config, spin_buf, thr_buf, sem, base):
    copies = [
        pltpu.make_async_copy(spins_ref.at[config], spin_buf, sem.at[base]),
        pltpu.make_async_copy(thr_ref.at[0, config], thr_buf.at[0], sem.at[base + 1]),
        pltpu.make_async_copy(thr_ref.at[1, config], thr_buf.at[1], sem.at[base + 2]),
    ]
    for copy in copies:
        copy.start()
    return copies


def scalars(beta_ref, coup_ref, beta_buf, coup_buf, sem, base):
    copies = [
        pltpu.make_async_copy(beta_ref, beta_buf, sem.at[base]),
        pltpu.make_async_copy(coup_ref, coup_buf, sem.at[base + 1]),
    ]
    for copy in copies:
        copy.start()
    return copies


def front_kernel(
    spins_ref, thr_ref, beta_ref, coup_ref, right_ref, down_ref,
    far_ref, near_ref, far_edge_ref, near_edge_ref, inner_edge_ref,
    edge_spins, edge_thr, spin_buf, thr_buf, right_buf, down_buf, beta_buf, coup_buf, sem,
):
    is_even = lax.rem(lax.axis_index("rep"), 2) == 0
    far, near = jnp.where(is_even, 0, 4), jnp.where(is_even, 4, 0)
    last = TILES - 1
    edge_copies = []
    for side in range(2):
        at = pl.ds(side * last * 128, 128)
        edge_copies.append(
            pltpu.make_async_copy(spins_ref.at[:, :, :, at], edge_spins.at[side], sem.at[side])
        )
        edge_copies.append(
            pltpu.make_async_copy(thr_ref.at[0, :, :, at], edge_thr.at[side], sem.at[2 + side])
        )
    edge_copies.append(pltpu.make_async_copy(right_ref, right_buf, sem.at[4]))
    edge_copies.append(pltpu.make_async_copy(down_ref, down_buf, sem.at[5]))
    for copy in edge_copies:
        copy.start()
    small = scalars(beta_ref, coup_ref, beta_buf, coup_buf, sem, 6)
    leaving = [
        fetch(spins_ref, thr_ref, config, spin_buf.at[n], thr_buf.at[n], sem, 8 + 3 * n)
        for n, config in enumerate((far, near))
    ]
    masks = (checker(), 7 - subs())
    for copy in edge_copies:
        copy.wait()
    bonds = 3 * EDGE
    inner_edge_ref[bonds] = jnp.zeros((8, 128), F32)
    inner_edge_ref[bonds, 0:1] = down_buf[0:1]
    inner_edge_ref[bonds, 1:2] = down_buf[last : last + 1]
    inner_edge_ref[bonds, 2:3] = right_buf[0:1]
    inner_edge_ref[bonds, 3:4] = right_buf[last : last + 1]
    for config, out, base in (
        (1, inner_edge_ref, 0), (2, inner_edge_ref, EDGE), (3, inner_edge_ref, 2 * EDGE),
        (near, near_edge_ref, 0), (far, far_edge_ref, 0),
    ):
        edge_message(
            lambda side, comp, half: edge_spins[side, config, comp, half * 8 : half * 8 + 8],
            lambda side, half: edge_thr[side, config, half * 8 : half * 8 + 8],
            masks, out, base,
        )
    far_edge_ref[EDGE] = jnp.zeros((8, 128), F32)
    for copy in small:
        copy.wait()
    for n, (config, out) in enumerate(((far, far_ref), (near, near_ref))):
        out[CORE] = jnp.full((8, 128), beta_buf[config], F32)
        out[CORE + 1] = jnp.full((8, 128), coup_buf[config], F32)
        for copy in leaving[n]:
            copy.wait()

        def put(plane, k, value):
            out[k * PLANES + plane] = value

        pack_config(*config_reader(spin_buf.at[n], thr_buf.at[n]), masks, put)


class Either:
    def __init__(self, first, ref, other):
        self.first, self.ref, self.other = first, ref, other

    def __getitem__(self, at):
        return jnp.where(self.first, self.ref[at], self.other[at])


def has_far():
    rep = lax.axis_index("rep")
    return jnp.logical_and(rep != 0, rep != lax.axis_size("rep") - 1)


def inner_kernel(
    spins_ref, thr_ref, beta_ref, coup_ref,
    inner_ref, rows_ref, scale_ref,
    spin_buf, thr_buf, beta_buf, coup_buf, sem,
):
    far = jnp.where(lax.rem(lax.axis_index("rep"), 2) == 0, 0, 4)
    copies = [
        fetch(spins_ref, thr_ref, config, spin_buf.at[n], thr_buf.at[n], sem, 3 * n)
        for n, config in enumerate((1, 2, 3, far))
    ]
    small = scalars(beta_ref, coup_ref, beta_buf, coup_buf, sem, 12)
    masks = (checker(), 7 - subs())
    for n in range(4):
        for copy in copies[n]:
            copy.wait()

        def put(plane, k, value):
            inner_ref[n, k * PLANES + plane] = value
            if n < 3 and plane < 7:
                rows_ref[plane * TILES + k, n : n + 1] = value[0:1]
            if n < 3 and 3 <= plane < 6:
                rows_ref[(plane + 4) * TILES + k, n : n + 1] = value[1:2]

        pack_config(*config_reader(spin_buf.at[n], thr_buf.at[n]), masks, put)
    for copy in small:
        copy.wait()
    sub = subs()
    for base, buf in ((0, beta_buf), (1, coup_buf)):
        scale_ref[base] = jnp.where(sub == 0, buf[1], jnp.where(sub == 1, buf[2], buf[3]))
        scale_ref[2 + base] = jnp.full((8, 128), buf[far], F32)


def slices_kernel(
    rows_ref, scale_ref, inner_ref, x_ref, y_ref, inner_edge_ref, x_edge_ref, y_edge_ref,
    up_ref, down_ref, own_ref,
):
    sub = subs()
    even = checker_row0(8)
    low = lanes() < 64
    swap = jnp.bitwise_xor(lanes(), 1)

    came = has_far()

    def five(mine, x, y):
        return jnp.where(sub == 3, x, jnp.where(sub == 4, y, mine))

    def row(q, k):
        plane, s = (q, 0) if q < 7 else (q - 4, 1)
        at = k * PLANES + plane
        y = jnp.where(came, y_ref[at, s : s + 1], inner_ref[3, at, s : s + 1])
        return five(rows_ref[q * TILES + k], x_ref[at, s : s + 1], y)

    for k in range(TILES):
        p0 = [row(c, k) for c in range(3)]
        p1 = [row(3 + c, k) for c in range(3)]
        w0 = row(6, k)
        second = [row(7 + c, k) for c in range(3)]
        for c in range(3):
            own_ref[k * 3 + c] = p1[c]
        swapped_y, swapped_w = take(second[1], swap, 1), take(w0, swap, 1)
        down = [jnp.where(even, p0[c], p1[c]) for c in range(3)]
        down += [jnp.where(even, second[0], swapped_y), jnp.where(even, second[2], swapped_w)]
        up = [jnp.where(even, p1[c], p0[c]) for c in range(3)]
        up += [jnp.where(even, swapped_y, second[0]), jnp.where(even, swapped_w, second[2])]
        for q in range(CHUNK):
            at = (k * CHUNK + q) * 5
            down_ref[at : at + 5] = down[q][0:5]
            up_ref[at : at + 5] = up[q][0:5]
    for c in range(3):
        merged = []
        for ref, base in ((inner_edge_ref, 0), (inner_edge_ref, EDGE), (inner_edge_ref, 2 * EDGE), (x_edge_ref, 0), (y_edge_ref, 0)):
            merged.append(jnp.where(low[0:1], ref[base + c, 0:1], ref[base + 3 + c, 0:1]))
        corner = five(
            jnp.where(sub == 0, merged[0], jnp.where(sub == 1, merged[1], merged[2])), merged[3], merged[4]
        )
        at = (TILES * CHUNK + c) * 5
        down_ref[at : at + 5] = corner[0:5]
        up_ref[at : at + 5] = corner[0:5]
    at = (TILES * CHUNK + 3) * 5
    down_ref[at:MESSAGE_ROWS] = jnp.zeros((MESSAGE_ROWS - at, 128), F32)
    up_ref[at:MESSAGE_ROWS] = jnp.zeros((MESSAGE_ROWS - at, 128), F32)
    for base in range(2):
        y = jnp.where(came, y_ref[CORE + base], scale_ref[2 + base])
        own_ref[3 * TILES + base] = five(scale_ref[base], x_ref[CORE + base], y)


def row_neighbours():
    lane = lanes()
    column = lax.rem(lane, 64)
    right = jnp.where(column == 63, lane - 63, lane + 1)
    left = jnp.where(column == 0, lane + 63, lane - 1)
    return right, left


def normalized(moved):
    scale = lax.rsqrt(0.25 + (moved[0] * moved[0] + moved[1] * moved[1] + moved[2] * moved[2]))
    return [m * scale for m in moved]


def edge_list(inner_edge_ref, x_edge_ref, y_edge_ref):
    inner = [(inner_edge_ref, n * EDGE) for n in range(3)]
    return inner + [(x_edge_ref, 0), (y_edge_ref, 0)]


def core_list(inner_ref, x_ref, y_ref):
    return [inner_ref.at[0], inner_ref.at[1], inner_ref.at[2], x_ref, Either(has_far(), y_ref, inner_ref.at[3])]


def space_field(bonds, at, above, here, turned, below, masks):
    low, right_at, left_at = masks
    return (
        bonds[at * 4] * jnp.where(low, turned, below)
        + bonds[at * 4 + 1] * jnp.where(low, above, turned)
        + bonds[at * 4 + 2] * take(here, right_at, 1)
        + bonds[at * 4 + 3] * take(here, left_at, 1)
    )


def turn(x):
    return pltpu.roll(x, 64, 1)


def prepare_kernel(
    inner_ref, x_ref, y_ref, inner_edge_ref, x_edge_ref, y_edge_ref, own_ref, right_ref, bdown_ref,
    moved_ref, bonds,
):
    low = lanes() < 64
    sub = subs()
    right_at, left_at = row_neighbours()
    masks = (low, right_at, left_at)
    edge_bonds = 3 * EDGE

    def bond_rows(k):
        if k == -1:
            return inner_edge_ref[edge_bonds, 1:2], inner_edge_ref[edge_bonds, 3:4]
        if k == TILES:
            return inner_edge_ref[edge_bonds, 0:1], inner_edge_ref[edge_bonds, 2:3]
        return bdown_ref[k : k + 1], right_ref[k : k + 1]

    before = jnp.zeros((8, 128), F32)
    for k in range(-1, TILES + 1):
        down, right = (jnp.broadcast_to(row, (8, 128)) for row in bond_rows(k))
        turned = turn(down)
        bonds[(k + 1) * 4] = down
        bonds[(k + 1) * 4 + 1] = jnp.where(low, before, turned)
        bonds[(k + 1) * 4 + 2] = right
        bonds[(k + 1) * 4 + 3] = take(right, left_at, 1)
        before = turned

    edges = edge_list(inner_edge_ref, x_edge_ref, y_edge_ref)
    for n, core in enumerate(core_list(inner_ref, x_ref, y_ref)):
        edge, base = edges[n]
        beta = jnp.broadcast_to(own_ref[3 * TILES, n : n + 1], (8, 128))
        coup = jnp.broadcast_to(own_ref[3 * TILES + 1, n : n + 1], (8, 128))

        def second(at, c):
            if at == 0:
                return edge[base + 3 + c]
            if at == TILES + 1:
                return edge[base + c]
            return core[(at - 1) * PLANES + 3 + c]

        here = [second(0, c) for c in range(3)]
        turned = [turn(x) for x in here]
        above = turned
        for at in range(TILES + 2):
            outer = at == 0 or at == TILES + 1
            if at <= TILES:
                following = [second(at + 1, c) for c in range(3)]
                below = [turn(x) for x in following]
            else:
                following, below = here, turned
            weight = edge[base + 9] if outer else core[(at - 1) * PLANES + 6]
            for c in range(3):
                x = here[c]
                space = space_field(bonds, at, above[c], x, turned[c], below[c], masks)
                inside = jnp.where(sub == 0, 0.0, pltpu.roll(x, 1, 0)) + jnp.where(sub == 7, x, pltpu.roll(x, 7, 0))
                mine = edge[base + 6 + c] if outer else core[(at - 1) * PLANES + c]
                moved_ref[n, at * 3 + c] = mine + weight * (beta * space + coup * inside)
            above, turned, here = turned, below, following


def sweep_kernel(
    inner_ref, x_ref, y_ref, inner_edge_ref, x_edge_ref, y_edge_ref, own_ref, moved_ref, bonds, up_ref, down_ref,
    partner_ref, accept_ref,
    final_ref, energy_ref,
    halo, halo_first,
):
    rep = lax.axis_index("rep")
    is_even = lax.rem(rep, 2) == 0
    low = lanes() < 64
    sub = subs()
    lane = lanes()
    mask = checker()
    right_at, left_at = row_neighbours()
    masks = (low, right_at, left_at)

    even8 = checker_row0(8)
    swap = jnp.bitwise_xor(lanes(), 1)

    def chunk(ref, i):
        at = i * 5
        return ref[at : at + 8]

    beta_rows = own_ref[3 * TILES]
    coup_rows = own_ref[3 * TILES + 1]
    for k in range(TILES):
        for c in range(3):
            up, down = chunk(up_ref, k * CHUNK + c), chunk(down_ref, k * CHUNK + c)
            halo[(k + 1) * 3 + c] = jnp.where(even8, up, down)
            halo_first[k * 3 + c] = jnp.where(even8, down, up)
    for c in range(3):
        corner = jnp.where(even8, chunk(up_ref, TILES * CHUNK + c), chunk(down_ref, TILES * CHUNK + c))
        halo[c] = corner
        halo[(TILES + 1) * 3 + c] = corner
    here = [halo[3 + c] for c in range(3)]
    above, turned = [turn(halo[c]) for c in range(3)], [turn(x) for x in here]
    for k in range(TILES):
        following = [halo[(k + 2) * 3 + c] for c in range(3)]
        below = [turn(x) for x in following]
        a_up, a_down = chunk(up_ref, k * CHUNK + 3), chunk(down_ref, k * CHUNK + 3)
        b_up, b_down = chunk(up_ref, k * CHUNK + 4), chunk(down_ref, k * CHUNK + 4)
        second = [
            jnp.where(even8, a_down, a_up),
            take(jnp.where(even8, a_up, a_down), swap, 1),
            jnp.where(even8, b_down, b_up),
        ]
        weight = take(jnp.where(even8, b_up, b_down), swap, 1)
        moved = []
        for c in range(3):
            field = beta_rows * space_field(bonds, k + 1, above[c], here[c], turned[c], below[c], masks)
            field = field + coup_rows * (own_ref[k * 3 + c] + second[c])
            moved.append(halo_first[k * 3 + c] + weight * field)
        fresh = normalized(moved)
        for c in range(3):
            halo_first[k * 3 + c] = fresh[c]
        above, turned, here = turned, below, following

    edges = edge_list(inner_edge_ref, x_edge_ref, y_edge_ref)
    energy_ref[...] = jnp.zeros((8, 128), F32)
    for n, core in enumerate(core_list(inner_ref, x_ref, y_ref)):
        edge, base = edges[n]
        beta = jnp.broadcast_to(own_ref[3 * TILES, n : n + 1], (8, 128))
        coup = jnp.broadcast_to(own_ref[3 * TILES + 1, n : n + 1], (8, 128))
        coup_outer = jnp.where(sub == 0, coup, 0.0)
        if n < 3:
            slot = n + 1
        elif n == 3:
            slot = jnp.where(is_even, 4, 0)
        else:
            slot = jnp.where(is_even, 0, 4)
        target = jnp.where(accept_ref[slot] == 1, jnp.clip(partner_ref[slot] - 5 * rep, 0, 4), slot)

        def pass_0(at):
            outer = at == 0 or at == TILES + 1
            factor = (edge[base + 9] if outer else core[(at - 1) * PLANES + 6]) * coup_outer
            fresh = normalized([
                moved_ref[n, at * 3 + c] + factor * halo[at * 3 + c, n : n + 1] for c in range(3)
            ])
            if not outer:
                for c in range(3):
                    final_ref[target, (at - 1) * 6 + c] = fresh[c]
            return fresh, [turn(x) for x in fresh]

        _, above = pass_0(0)
        here, turned = pass_0(1)
        total = jnp.zeros((8, 128), F32)
        for k in range(TILES):
            following, below = pass_0(k + 2)
            weight = core[k * PLANES + 7]
            fields, moved = [], []
            for c in range(3):
                x = here[c]
                space = space_field(bonds, k + 1, above[c], x, turned[c], below[c], masks)
                outside = halo_first[k * 3 + c, n : n + 1]
                around = jnp.where(sub == 0, outside, pltpu.roll(x, 1, 0)) + jnp.where(sub == 7, x, pltpu.roll(x, 7, 0))
                moved.append(core[k * PLANES + 3 + c] + weight * (beta * space + coup * around))
                fields.append(space)
            fresh = normalized(moved)
            total = total + (fresh[0] * fields[0] + fresh[1] * fields[1] + fresh[2] * fields[2])
            for c in range(3):
                final_ref[target, k * 6 + 3 + c] = fresh[c]
            above, turned, here = turned, below, following
        head = jnp.sum(jnp.where(mask, 0.0, total), axis=1, keepdims=True)
        back = jnp.sum(jnp.where(mask, total, 0.0), axis=1, keepdims=True)
        line = jnp.where(lane == sub, head, 0.0) + jnp.where(lane == 15 - sub, back, 0.0)
        line = jnp.sum(line, axis=0, keepdims=True)
        energy_ref[...] = jnp.where(sub == target, -line / 4096.0, energy_ref[...])


def unpack_kernel(final_ref, out_ref, out_buf, sem):
    mask = checker()
    flip = 7 - subs()
    writes = []
    for n in range(5):
        for k in range(TILES):
            for c in range(3):
                p0, p1 = final_ref[n, k * 6 + c], final_ref[n, k * 6 + 3 + c]
                out_buf[n, c, 0:8, k * 128 : k * 128 + 128] = jnp.where(mask, p0, p1)
                out_buf[n, c, 8:16, k * 128 : k * 128 + 128] = take(jnp.where(mask, p1, p0), flip, 0)
        write = pltpu.make_async_copy(out_buf.at[n], out_ref.at[n], sem.at[n])
        write.start()
        writes.append(write)
    for write in writes:
        write.wait()


def params(limit=VMEM_LIMIT):
    return pltpu.CompilerParams(vmem_limit_bytes=limit)


def vmem():
    return pl.BlockSpec(memory_space=pltpu.VMEM)


def smem():
    return pl.BlockSpec(memory_space=pltpu.SMEM)


def hbm():
    return pl.BlockSpec(memory_space=pltpu.HBM)


def anywhere():
    return pl.BlockSpec(memory_space=pl.ANY)


def shape(*dims):
    return jax.ShapeDtypeStruct(dims, F32)


def on_device(spins, bond_right, bond_down, betas, time_coupling, thresholds, partner, accept):
    ranks, depth = lax.axis_size("rep"), lax.axis_size("tm")
    axes = ("rep", "tm", "space")
    right, down = bond_right.reshape(TILES, 128), bond_down.reshape(TILES, 128)

    def far_of(r):
        other = r - 1 if r % 2 == 0 else r + 1
        return other if 0 <= other < ranks else r

    def near_of(r):
        return r + 1 if r % 2 == 0 else r - 1

    def crosswise(x, of):
        pairs = [
            ((r * depth + t) * 2 + s, (of(r) * depth + t) * 2 + 1 - s)
            for r in range(ranks) for t in range(depth) for s in range(2)
        ]
        return lax.ppermute(x, axes, pairs)

    far_core, near_core, far_edge, near_edge, inner_edge = pl.pallas_call(
        front_kernel,
        out_shape=(
            shape(CORE_MSG, 8, 128), shape(CORE_MSG, 8, 128),
            shape(FAR_EDGE, 8, 128), shape(EDGE, 8, 128), shape(3 * EDGE + 1, 8, 128),
        ),
        in_specs=[hbm()] * 6,
        out_specs=(vmem(),) * 5,
        scratch_shapes=[
            pltpu.VMEM((2, 5, 3, 16, 128), F32),
            pltpu.VMEM((2, 5, 16, 128), jnp.int32),
            pltpu.VMEM((2, 3, 16, 2048), F32),
            pltpu.VMEM((2, 2, 16, 2048), jnp.int32),
            pltpu.VMEM((TILES, 128), F32),
            pltpu.VMEM((TILES, 128), F32),
            pltpu.SMEM((5,), F32),
            pltpu.SMEM((5,), F32),
            pltpu.SemaphoreType.DMA((14,)),
        ],
        compiler_params=params(FRONT_LIMIT),
        name="front",
    )(spins, thresholds, betas, time_coupling, right, down)
    far_core = lax.ppermute(far_core, "rep", [(r, far_of(r)) for r in range(ranks) if far_of(r) != r])
    inner_edge = lax.ppermute(inner_edge, "space", [(0, 1), (1, 0)])
    far_edge = crosswise(far_edge, far_of)
    near_edge = crosswise(near_edge, near_of)
    near_core = lax.ppermute(near_core, "rep", [(r, near_of(r)) for r in range(ranks)])

    inner, rows, scale = pl.pallas_call(
        inner_kernel,
        out_shape=(shape(4, CORE, 8, 128), shape(ROWQ * TILES, 8, 128), shape(4, 8, 128)),
        in_specs=[hbm()] * 4,
        out_specs=(vmem(),) * 3,
        scratch_shapes=[
            pltpu.VMEM((4, 3, 16, 2048), F32),
            pltpu.VMEM((4, 2, 16, 2048), jnp.int32),
            pltpu.SMEM((5,), F32),
            pltpu.SMEM((5,), F32),
            pltpu.SemaphoreType.DMA((14,)),
        ],
        compiler_params=params(INNER_LIMIT),
        name="pack_inner",
    )(spins, thresholds, betas, time_coupling)

    message = shape(MESSAGE_ROWS, 128)
    up, down_msg, own = pl.pallas_call(
        slices_kernel,
        out_shape=(message, message, shape(3 * TILES + 2, 8, 128)),
        in_specs=[vmem()] * 8,
        out_specs=(vmem(),) * 3,
        compiler_params=params(),
        name="slices",
    )(rows, scale, inner, near_core, far_core, inner_edge, near_edge, far_edge)
    from_before = lax.ppermute(up, "tm", [(t, (t + 1) % depth) for t in range(depth)])
    from_after = lax.ppermute(down_msg, "tm", [((t + 1) % depth, t) for t in range(depth)])

    edges = (inner_edge, near_edge, far_edge)
    moved, bonds = pl.pallas_call(
        prepare_kernel,
        out_shape=(shape(5, (TILES + 2) * 3, 8, 128), shape((TILES + 2) * 4, 8, 128)),
        in_specs=[vmem()] * 9,
        out_specs=(vmem(),) * 2,
        compiler_params=params(),
        name="prepare",
    )(inner, near_core, far_core, *edges, own, right, down)
    final, energy = pl.pallas_call(
        sweep_kernel,
        out_shape=(shape(5, TILES * 6, 8, 128), shape(8, 128)),
        in_specs=[vmem()] * 11 + [smem()] * 2,
        out_specs=(vmem(),) * 2,
        scratch_shapes=[
            pltpu.VMEM(((TILES + 2) * 3, 8, 128), F32),
            pltpu.VMEM((TILES * 3, 8, 128), F32),
        ],
        compiler_params=params(),
        name="sweep",
    )(
        inner, near_core, far_core, *edges, own, moved, bonds, from_before, from_after, partner, accept,
    )
    other_energy = lax.ppermute(energy, "space", [(0, 1), (1, 0)])
    swapped = pl.pallas_call(
        unpack_kernel,
        out_shape=shape(5, 3, 16, 2048),
        in_specs=[vmem()],
        out_specs=hbm(),
        scratch_shapes=[pltpu.VMEM((5, 3, 16, 2048), F32), pltpu.SemaphoreType.DMA((5,))],
        compiler_params=params(),
        name="unpack",
    )(final)
    energy = energy + other_energy
    return swapped, energy[:5, :16]


def solution(mesh):
    placed = (
        P("rep", None, "tm", "space"),
        P("space"),
        P("space"),
        P("rep"),
        P("rep"),
        P(None, "rep", "tm", "space"),
        P("rep"),
        P("rep"),
    )
    return jax.shard_map(
        on_device,
        mesh=mesh,
        in_specs=placed,
        out_specs=(P("rep", None, "tm", "space"), P("rep", "tm")),
        check_vma=False,
    )
```

```python
import jax
import jax.numpy as jnp
from jax import lax
from jax.experimental import pallas as pl
from jax.experimental.pallas import tpu as pltpu
from jax.sharding import PartitionSpec as P

TILES = 16
PLANES = 8
CORE = TILES * PLANES
CORE_MSG = CORE + 2
EDGE = 10
FAR_EDGE = EDGE + 1
ROWQ = 10
MESSAGE_ROWS = 424
CHUNK = 5
F32 = jnp.float32
VMEM_LIMIT = 16 * 1024 * 1024
FRONT_LIMIT = 61 * 1024 * 1024
INNER_LIMIT = 16 * 1024 * 1024


def lanes():
    return lax.broadcasted_iota(jnp.int32, (8, 128), 1)


def subs():
    return lax.broadcasted_iota(jnp.int32, (8, 128), 0)


def checker():
    lane = lanes()
    return lax.rem(lane // 64 + lax.rem(lane, 64) + subs(), 2) == 0


def checker_row0(rows):
    lane = lax.broadcasted_iota(jnp.int32, (rows, 128), 1)
    return lax.rem(lane // 64 + lax.rem(lane, 64), 2) == 0


def take(x, index, axis):
    return jnp.take_along_axis(x, index, axis=axis, mode="promise_in_bounds")


def pack_config(spins, thr0, thr1, masks, put):
    mask, flip = masks
    for k in range(TILES):
        for comp in range(3):
            a, b = spins(comp, 0, k), take(spins(comp, 1, k), flip, 0)
            put(comp, k, jnp.where(mask, a, b))
            put(3 + comp, k, jnp.where(mask, b, a))
        a, b = thr0(0, k), take(thr0(1, k), flip, 0)
        put(6, k, (jnp.where(mask, a, b).astype(F32) + 0.5) / 8192.0)
        a, b = thr1(0, k), take(thr1(1, k), flip, 0)
        put(7, k, (jnp.where(mask, b, a).astype(F32) + 0.5) / 8192.0)


def config_reader(spin_buf, thr_buf):
    def spins(comp, half, k):
        return spin_buf[comp, half * 8 : half * 8 + 8, k * 128 : k * 128 + 128]

    def thr(which):
        return lambda half, k: thr_buf[which, half * 8 : half * 8 + 8, k * 128 : k * 128 + 128]

    return spins, thr(0), thr(1)


def edge_message(spins, thr, masks, out, base):
    mask, flip = masks
    low = lanes() < 64
    for comp in range(3):
        own = []
        for side in range(2):
            a, b = spins(side, comp, 0), take(spins(side, comp, 1), flip, 0)
            own.append(jnp.where(mask, a, b))
            out[base + 3 * side + comp] = jnp.where(mask, b, a)
        out[base + 6 + comp] = jnp.where(low, own[0], own[1])
    steps = [jnp.where(mask, thr(side, 0), take(thr(side, 1), flip, 0)) for side in range(2)]
    out[base + 9] = (jnp.where(low, steps[0], steps[1]).astype(F32) + 0.5) / 8192.0


def fetch(spins_ref, thr_ref, config, spin_buf, thr_buf, sem, base):
    copies = [
        pltpu.make_async_copy(spins_ref.at[config], spin_buf, sem.at[base]),
        pltpu.make_async_copy(thr_ref.at[0, config], thr_buf.at[0], sem.at[base + 1]),
        pltpu.make_async_copy(thr_ref.at[1, config], thr_buf.at[1], sem.at[base + 2]),
    ]
    for copy in copies:
        copy.start()
    return copies


def scalars(beta_ref, coup_ref, beta_buf, coup_buf, sem, base):
    copies = [
        pltpu.make_async_copy(beta_ref, beta_buf, sem.at[base]),
        pltpu.make_async_copy(coup_ref, coup_buf, sem.at[base + 1]),
    ]
    for copy in copies:
        copy.start()
    return copies


def front_kernel(
    spins_ref, thr_ref, beta_ref, coup_ref, right_ref, down_ref,
    far_ref, near_ref, far_edge_ref, near_edge_ref, inner_edge_ref,
    edge_spins, edge_thr, spin_buf, thr_buf, right_buf, down_buf, beta_buf, coup_buf, sem,
):
    is_even = lax.rem(lax.axis_index("rep"), 2) == 0
    far, near = jnp.where(is_even, 0, 4), jnp.where(is_even, 4, 0)
    last = TILES - 1
    edge_copies = []
    for side in range(2):
        at = pl.ds(side * last * 128, 128)
        edge_copies.append(
            pltpu.make_async_copy(spins_ref.at[:, :, :, at], edge_spins.at[side], sem.at[side])
        )
        edge_copies.append(
            pltpu.make_async_copy(thr_ref.at[0, :, :, at], edge_thr.at[side], sem.at[2 + side])
        )
    edge_copies.append(pltpu.make_async_copy(right_ref, right_buf, sem.at[4]))
    edge_copies.append(pltpu.make_async_copy(down_ref, down_buf, sem.at[5]))
    for copy in edge_copies:
        copy.start()
    small = scalars(beta_ref, coup_ref, beta_buf, coup_buf, sem, 6)
    leaving = [
        fetch(spins_ref, thr_ref, config, spin_buf.at[n], thr_buf.at[n], sem, 8 + 3 * n)
        for n, config in enumerate((far, near))
    ]
    masks = (checker(), 7 - subs())
    for copy in edge_copies:
        copy.wait()
    bonds = 3 * EDGE
    inner_edge_ref[bonds] = jnp.zeros((8, 128), F32)
    inner_edge_ref[bonds, 0:1] = down_buf[0:1]
    inner_edge_ref[bonds, 1:2] = down_buf[last : last + 1]
    inner_edge_ref[bonds, 2:3] = right_buf[0:1]
    inner_edge_ref[bonds, 3:4] = right_buf[last : last + 1]
    for config, out, base in (
        (1, inner_edge_ref, 0), (2, inner_edge_ref, EDGE), (3, inner_edge_ref, 2 * EDGE),
        (near, near_edge_ref, 0), (far, far_edge_ref, 0),
    ):
        edge_message(
            lambda side, comp, half: edge_spins[side, config, comp, half * 8 : half * 8 + 8],
            lambda side, half: edge_thr[side, config, half * 8 : half * 8 + 8],
            masks, out, base,
        )
    far_edge_ref[EDGE] = jnp.zeros((8, 128), F32)
    for copy in small:
        copy.wait()
    for n, (config, out) in enumerate(((far, far_ref), (near, near_ref))):
        out[CORE] = jnp.full((8, 128), beta_buf[config], F32)
        out[CORE + 1] = jnp.full((8, 128), coup_buf[config], F32)
        for copy in leaving[n]:
            copy.wait()

        def put(plane, k, value):
            out[k * PLANES + plane] = value

        pack_config(*config_reader(spin_buf.at[n], thr_buf.at[n]), masks, put)


class Either:
    def __init__(self, first, ref, other):
        self.first, self.ref, self.other = first, ref, other

    def __getitem__(self, at):
        return jnp.where(self.first, self.ref[at], self.other[at])


def has_far():
    rep = lax.axis_index("rep")
    return jnp.logical_and(rep != 0, rep != lax.axis_size("rep") - 1)


def inner_kernel(
    spins_ref, thr_ref, beta_ref, coup_ref,
    inner_ref, rows_ref, scale_ref,
    spin_buf, thr_buf, beta_buf, coup_buf, sem,
):
    far = jnp.where(lax.rem(lax.axis_index("rep"), 2) == 0, 0, 4)
    copies = [
        fetch(spins_ref, thr_ref, config, spin_buf.at[n], thr_buf.at[n], sem, 3 * n)
        for n, config in enumerate((1, 2, 3))
    ]
    small = scalars(beta_ref, coup_ref, beta_buf, coup_buf, sem, 12)
    masks = (checker(), 7 - subs())
    for n in range(3):
        for copy in copies[n]:
            copy.wait()

        def put(plane, k, value):
            inner_ref[n, k * PLANES + plane] = value
            if plane < 7:
                rows_ref[plane * TILES + k, n : n + 1] = value[0:1]
            if 3 <= plane < 6:
                rows_ref[(plane + 4) * TILES + k, n : n + 1] = value[1:2]

        pack_config(*config_reader(spin_buf.at[n], thr_buf.at[n]), masks, put)
    for copy in small:
        copy.wait()
    sub = subs()
    for base, buf in ((0, beta_buf), (1, coup_buf)):
        scale_ref[base] = jnp.where(sub == 0, buf[1], jnp.where(sub == 1, buf[2], buf[3]))
        scale_ref[2 + base] = jnp.full((8, 128), buf[far], F32)

    @pl.when(jnp.logical_not(has_far()))
    def _():
        for copy in fetch(spins_ref, thr_ref, far, spin_buf.at[3], thr_buf.at[3], sem, 9):
            copy.wait()

        def put_far(plane, k, value):
            inner_ref[3, k * PLANES + plane] = value

        pack_config(*config_reader(spin_buf.at[3], thr_buf.at[3]), masks, put_far)


def slices_kernel(
    rows_ref, scale_ref, inner_ref, x_ref, y_ref, inner_edge_ref, x_edge_ref, y_edge_ref,
    up_ref, down_ref, own_ref,
):
    sub = subs()
    even = checker_row0(8)
    low = lanes() < 64
    swap = jnp.bitwise_xor(lanes(), 1)

    came = has_far()

    def five(mine, x, y):
        return jnp.where(sub == 3, x, jnp.where(sub == 4, y, mine))

    def row(q, k):
        plane, s = (q, 0) if q < 7 else (q - 4, 1)
        at = k * PLANES + plane
        y = jnp.where(came, y_ref[at, s : s + 1], inner_ref[3, at, s : s + 1])
        return five(rows_ref[q * TILES + k], x_ref[at, s : s + 1], y)

    for k in range(TILES):
        p0 = [row(c, k) for c in range(3)]
        p1 = [row(3 + c, k) for c in range(3)]
        w0 = row(6, k)
        second = [row(7 + c, k) for c in range(3)]
        for c in range(3):
            own_ref[k * 3 + c] = p1[c]
        swapped_y, swapped_w = take(second[1], swap, 1), take(w0, swap, 1)
        down = [jnp.where(even, p0[c], p1[c]) for c in range(3)]
        down += [jnp.where(even, second[0], swapped_y), jnp.where(even, second[2], swapped_w)]
        up = [jnp.where(even, p1[c], p0[c]) for c in range(3)]
        up += [jnp.where(even, swapped_y, second[0]), jnp.where(even, swapped_w, second[2])]
        for q in range(CHUNK):
            at = (k * CHUNK + q) * 5
            down_ref[at : at + 5] = down[q][0:5]
            up_ref[at : at + 5] = up[q][0:5]
    for c in range(3):
        merged = []
        for ref, base in ((inner_edge_ref, 0), (inner_edge_ref, EDGE), (inner_edge_ref, 2 * EDGE), (x_edge_ref, 0), (y_edge_ref, 0)):
            merged.append(jnp.where(low[0:1], ref[base + c, 0:1], ref[base + 3 + c, 0:1]))
        corner = five(
            jnp.where(sub == 0, merged[0], jnp.where(sub == 1, merged[1], merged[2])), merged[3], merged[4]
        )
        at = (TILES * CHUNK + c) * 5
        down_ref[at : at + 5] = corner[0:5]
        up_ref[at : at + 5] = corner[0:5]
    at = (TILES * CHUNK + 3) * 5
    down_ref[at:MESSAGE_ROWS] = jnp.zeros((MESSAGE_ROWS - at, 128), F32)
    up_ref[at:MESSAGE_ROWS] = jnp.zeros((MESSAGE_ROWS - at, 128), F32)
    for base in range(2):
        y = jnp.where(came, y_ref[CORE + base], scale_ref[2 + base])
        own_ref[3 * TILES + base] = five(scale_ref[base], x_ref[CORE + base], y)


def row_neighbours():
    lane = lanes()
    column = lax.rem(lane, 64)
    right = jnp.where(column == 63, lane - 63, lane + 1)
    left = jnp.where(column == 0, lane + 63, lane - 1)
    return right, left


def normalized(moved):
    scale = lax.rsqrt(0.25 + (moved[0] * moved[0] + moved[1] * moved[1] + moved[2] * moved[2]))
    return [m * scale for m in moved]


def edge_list(inner_edge_ref, x_edge_ref, y_edge_ref):
    inner = [(inner_edge_ref, n * EDGE) for n in range(3)]
    return inner + [(x_edge_ref, 0), (y_edge_ref, 0)]


def core_list(inner_ref, x_ref, y_ref):
    return [inner_ref.at[0], inner_ref.at[1], inner_ref.at[2], x_ref, Either(has_far(), y_ref, inner_ref.at[3])]


def space_field(bonds, at, above, here, turned, below, masks):
    low, right_at, left_at = masks
    return (
        bonds[at * 4] * jnp.where(low, turned, below)
        + bonds[at * 4 + 1] * jnp.where(low, above, turned)
        + bonds[at * 4 + 2] * take(here, right_at, 1)
        + bonds[at * 4 + 3] * take(here, left_at, 1)
    )


def turn(x):
    return pltpu.roll(x, 64, 1)


def prepare_kernel(
    inner_ref, x_ref, y_ref, inner_edge_ref, x_edge_ref, y_edge_ref, own_ref, right_ref, bdown_ref,
    moved_ref, bonds,
):
    low = lanes() < 64
    sub = subs()
    right_at, left_at = row_neighbours()
    masks = (low, right_at, left_at)
    edge_bonds = 3 * EDGE

    def bond_rows(k):
        if k == -1:
            return inner_edge_ref[edge_bonds, 1:2], inner_edge_ref[edge_bonds, 3:4]
        if k == TILES:
            return inner_edge_ref[edge_bonds, 0:1], inner_edge_ref[edge_bonds, 2:3]
        return bdown_ref[k : k + 1], right_ref[k : k + 1]

    before = jnp.zeros((8, 128), F32)
    for k in range(-1, TILES + 1):
        down, right = (jnp.broadcast_to(row, (8, 128)) for row in bond_rows(k))
        turned = turn(down)
        bonds[(k + 1) * 4] = down
        bonds[(k + 1) * 4 + 1] = jnp.where(low, before, turned)
        bonds[(k + 1) * 4 + 2] = right
        bonds[(k + 1) * 4 + 3] = take(right, left_at, 1)
        before = turned

    edges = edge_list(inner_edge_ref, x_edge_ref, y_edge_ref)
    for n, core in enumerate(core_list(inner_ref, x_ref, y_ref)):
        edge, base = edges[n]
        beta = jnp.broadcast_to(own_ref[3 * TILES, n : n + 1], (8, 128))
        coup = jnp.broadcast_to(own_ref[3 * TILES + 1, n : n + 1], (8, 128))

        def second(at, c):
            if at == 0:
                return edge[base + 3 + c]
            if at == TILES + 1:
                return edge[base + c]
            return core[(at - 1) * PLANES + 3 + c]

        here = [second(0, c) for c in range(3)]
        turned = [turn(x) for x in here]
        above = turned
        for at in range(TILES + 2):
            outer = at == 0 or at == TILES + 1
            if at <= TILES:
                following = [second(at + 1, c) for c in range(3)]
                below = [turn(x) for x in following]
            else:
                following, below = here, turned
            weight = edge[base + 9] if outer else core[(at - 1) * PLANES + 6]
            for c in range(3):
                x = here[c]
                space = space_field(bonds, at, above[c], x, turned[c], below[c], masks)
                inside = jnp.where(sub == 0, 0.0, pltpu.roll(x, 1, 0)) + jnp.where(sub == 7, x, pltpu.roll(x, 7, 0))
                mine = edge[base + 6 + c] if outer else core[(at - 1) * PLANES + c]
                moved_ref[n, at * 3 + c] = mine + weight * (beta * space + coup * inside)
            above, turned, here = turned, below, following


def sweep_kernel(
    inner_ref, x_ref, y_ref, inner_edge_ref, x_edge_ref, y_edge_ref, own_ref, moved_ref, bonds, up_ref, down_ref,
    partner_ref, accept_ref,
    final_ref, energy_ref,
    halo, halo_first,
):
    rep = lax.axis_index("rep")
    is_even = lax.rem(rep, 2) == 0
    low = lanes() < 64
    sub = subs()
    lane = lanes()
    mask = checker()
    right_at, left_at = row_neighbours()
    masks = (low, right_at, left_at)

    even8 = checker_row0(8)
    swap = jnp.bitwise_xor(lanes(), 1)

    def chunk(ref, i):
        at = i * 5
        return ref[at : at + 8]

    beta_rows = own_ref[3 * TILES]
    coup_rows = own_ref[3 * TILES + 1]
    for k in range(TILES):
        for c in range(3):
            up, down = chunk(up_ref, k * CHUNK + c), chunk(down_ref, k * CHUNK + c)
            halo[(k + 1) * 3 + c] = jnp.where(even8, up, down)
            halo_first[k * 3 + c] = jnp.where(even8, down, up)
    for c in range(3):
        corner = jnp.where(even8, chunk(up_ref, TILES * CHUNK + c), chunk(down_ref, TILES * CHUNK + c))
        halo[c] = corner
        halo[(TILES + 1) * 3 + c] = corner
    here = [halo[3 + c] for c in range(3)]
    above, turned = [turn(halo[c]) for c in range(3)], [turn(x) for x in here]
    for k in range(TILES):
        following = [halo[(k + 2) * 3 + c] for c in range(3)]
        below = [turn(x) for x in following]
        a_up, a_down = chunk(up_ref, k * CHUNK + 3), chunk(down_ref, k * CHUNK + 3)
        b_up, b_down = chunk(up_ref, k * CHUNK + 4), chunk(down_ref, k * CHUNK + 4)
        second = [
            jnp.where(even8, a_down, a_up),
            take(jnp.where(even8, a_up, a_down), swap, 1),
            jnp.where(even8, b_down, b_up),
        ]
        weight = take(jnp.where(even8, b_up, b_down), swap, 1)
        moved = []
        for c in range(3):
            field = beta_rows * space_field(bonds, k + 1, above[c], here[c], turned[c], below[c], masks)
            field = field + coup_rows * (own_ref[k * 3 + c] + second[c])
            moved.append(halo_first[k * 3 + c] + weight * field)
        fresh = normalized(moved)
        for c in range(3):
            halo_first[k * 3 + c] = fresh[c]
        above, turned, here = turned, below, following

    edges = edge_list(inner_edge_ref, x_edge_ref, y_edge_ref)
    energy_ref[...] = jnp.zeros((8, 128), F32)
    for n, core in enumerate(core_list(inner_ref, x_ref, y_ref)):
        edge, base = edges[n]
        beta = jnp.broadcast_to(own_ref[3 * TILES, n : n + 1], (8, 128))
        coup = jnp.broadcast_to(own_ref[3 * TILES + 1, n : n + 1], (8, 128))
        coup_outer = jnp.where(sub == 0, coup, 0.0)
        if n < 3:
            slot = n + 1
        elif n == 3:
            slot = jnp.where(is_even, 4, 0)
        else:
            slot = jnp.where(is_even, 0, 4)
        target = jnp.where(accept_ref[slot] == 1, jnp.clip(partner_ref[slot] - 5 * rep, 0, 4), slot)

        def pass_0(at):
            outer = at == 0 or at == TILES + 1
            factor = (edge[base + 9] if outer else core[(at - 1) * PLANES + 6]) * coup_outer
            fresh = normalized([
                moved_ref[n, at * 3 + c] + factor * halo[at * 3 + c, n : n + 1] for c in range(3)
            ])
            if not outer:
                for c in range(3):
                    final_ref[target, (at - 1) * 6 + c] = fresh[c]
            return fresh, [turn(x) for x in fresh]

        _, above = pass_0(0)
        here, turned = pass_0(1)
        total = jnp.zeros((8, 128), F32)
        for k in range(TILES):
            following, below = pass_0(k + 2)
            weight = core[k * PLANES + 7]
            fields, moved = [], []
            for c in range(3):
                x = here[c]
                space = space_field(bonds, k + 1, above[c], x, turned[c], below[c], masks)
                outside = halo_first[k * 3 + c, n : n + 1]
                around = jnp.where(sub == 0, outside, pltpu.roll(x, 1, 0)) + jnp.where(sub == 7, x, pltpu.roll(x, 7, 0))
                moved.append(core[k * PLANES + 3 + c] + weight * (beta * space + coup * around))
                fields.append(space)
            fresh = normalized(moved)
            total = total + (fresh[0] * fields[0] + fresh[1] * fields[1] + fresh[2] * fields[2])
            for c in range(3):
                final_ref[target, k * 6 + 3 + c] = fresh[c]
            above, turned, here = turned, below, following
        head = jnp.sum(jnp.where(mask, 0.0, total), axis=1, keepdims=True)
        back = jnp.sum(jnp.where(mask, total, 0.0), axis=1, keepdims=True)
        line = jnp.where(lane == sub, head, 0.0) + jnp.where(lane == 15 - sub, back, 0.0)
        line = jnp.sum(line, axis=0, keepdims=True)
        energy_ref[...] = jnp.where(sub == target, -line / 4096.0, energy_ref[...])


def unpack_kernel(final_ref, out_ref, out_buf, sem):
    mask = checker()
    flip = 7 - subs()
    writes = []
    for n in range(5):
        for k in range(TILES):
            for c in range(3):
                p0, p1 = final_ref[n, k * 6 + c], final_ref[n, k * 6 + 3 + c]
                out_buf[n, c, 0:8, k * 128 : k * 128 + 128] = jnp.where(mask, p0, p1)
                out_buf[n, c, 8:16, k * 128 : k * 128 + 128] = take(jnp.where(mask, p1, p0), flip, 0)
        write = pltpu.make_async_copy(out_buf.at[n], out_ref.at[n], sem.at[n])
        write.start()
        writes.append(write)
    for write in writes:
        write.wait()


def params(limit=VMEM_LIMIT):
    return pltpu.CompilerParams(vmem_limit_bytes=limit)


def vmem():
    return pl.BlockSpec(memory_space=pltpu.VMEM)


def smem():
    return pl.BlockSpec(memory_space=pltpu.SMEM)


def hbm():
    return pl.BlockSpec(memory_space=pltpu.HBM)


def anywhere():
    return pl.BlockSpec(memory_space=pl.ANY)


def shape(*dims):
    return jax.ShapeDtypeStruct(dims, F32)


def on_device(spins, bond_right, bond_down, betas, time_coupling, thresholds, partner, accept):
    ranks, depth = lax.axis_size("rep"), lax.axis_size("tm")
    axes = ("rep", "tm", "space")
    right, down = bond_right.reshape(TILES, 128), bond_down.reshape(TILES, 128)

    def far_of(r):
        other = r - 1 if r % 2 == 0 else r + 1
        return other if 0 <= other < ranks else r

    def near_of(r):
        return r + 1 if r % 2 == 0 else r - 1

    def crosswise(x, of):
        pairs = [
            ((r * depth + t) * 2 + s, (of(r) * depth + t) * 2 + 1 - s)
            for r in range(ranks) for t in range(depth) for s in range(2)
        ]
        return lax.ppermute(x, axes, pairs)

    far_core, near_core, far_edge, near_edge, inner_edge = pl.pallas_call(
        front_kernel,
        out_shape=(
            shape(CORE_MSG, 8, 128), shape(CORE_MSG, 8, 128),
            shape(FAR_EDGE, 8, 128), shape(EDGE, 8, 128), shape(3 * EDGE + 1, 8, 128),
        ),
        in_specs=[hbm()] * 6,
        out_specs=(vmem(),) * 5,
        scratch_shapes=[
            pltpu.VMEM((2, 5, 3, 16, 128), F32),
            pltpu.VMEM((2, 5, 16, 128), jnp.int32),
            pltpu.VMEM((2, 3, 16, 2048), F32),
            pltpu.VMEM((2, 2, 16, 2048), jnp.int32),
            pltpu.VMEM((TILES, 128), F32),
            pltpu.VMEM((TILES, 128), F32),
            pltpu.SMEM((5,), F32),
            pltpu.SMEM((5,), F32),
            pltpu.SemaphoreType.DMA((14,)),
        ],
        compiler_params=params(FRONT_LIMIT),
        name="front",
    )(spins, thresholds, betas, time_coupling, right, down)
    far_core = lax.ppermute(far_core, "rep", [(r, far_of(r)) for r in range(ranks) if far_of(r) != r])
    inner_edge = lax.ppermute(inner_edge, "space", [(0, 1), (1, 0)])
    far_edge = crosswise(far_edge, far_of)
    near_edge = crosswise(near_edge, near_of)
    near_core = lax.ppermute(near_core, "rep", [(r, near_of(r)) for r in range(ranks)])

    inner, rows, scale = pl.pallas_call(
        inner_kernel,
        out_shape=(shape(4, CORE, 8, 128), shape(ROWQ * TILES, 8, 128), shape(4, 8, 128)),
        in_specs=[hbm()] * 4,
        out_specs=(vmem(),) * 3,
        scratch_shapes=[
            pltpu.VMEM((4, 3, 16, 2048), F32),
            pltpu.VMEM((4, 2, 16, 2048), jnp.int32),
            pltpu.SMEM((5,), F32),
            pltpu.SMEM((5,), F32),
            pltpu.SemaphoreType.DMA((14,)),
        ],
        compiler_params=params(INNER_LIMIT),
        name="pack_inner",
    )(spins, thresholds, betas, time_coupling)

    message = shape(MESSAGE_ROWS, 128)
    up, down_msg, own = pl.pallas_call(
        slices_kernel,
        out_shape=(message, message, shape(3 * TILES + 2, 8, 128)),
        in_specs=[vmem()] * 8,
        out_specs=(vmem(),) * 3,
        compiler_params=params(),
        name="slices",
    )(rows, scale, inner, near_core, far_core, inner_edge, near_edge, far_edge)
    from_before = lax.ppermute(up, "tm", [(t, (t + 1) % depth) for t in range(depth)])
    from_after = lax.ppermute(down_msg, "tm", [((t + 1) % depth, t) for t in range(depth)])

    edges = (inner_edge, near_edge, far_edge)
    moved, bonds = pl.pallas_call(
        prepare_kernel,
        out_shape=(shape(5, (TILES + 2) * 3, 8, 128), shape((TILES + 2) * 4, 8, 128)),
        in_specs=[vmem()] * 9,
        out_specs=(vmem(),) * 2,
        compiler_params=params(),
        name="prepare",
    )(inner, near_core, far_core, *edges, own, right, down)
    final, energy = pl.pallas_call(
        sweep_kernel,
        out_shape=(shape(5, TILES * 6, 8, 128), shape(8, 128)),
        in_specs=[vmem()] * 11 + [smem()] * 2,
        out_specs=(vmem(),) * 2,
        scratch_shapes=[
            pltpu.VMEM(((TILES + 2) * 3, 8, 128), F32),
            pltpu.VMEM((TILES * 3, 8, 128), F32),
        ],
        compiler_params=params(),
        name="sweep",
    )(
        inner, near_core, far_core, *edges, own, moved, bonds, from_before, from_after, partner, accept,
    )
    other_energy = lax.ppermute(energy, "space", [(0, 1), (1, 0)])
    swapped = pl.pallas_call(
        unpack_kernel,
        out_shape=shape(5, 3, 16, 2048),
        in_specs=[vmem()],
        out_specs=hbm(),
        scratch_shapes=[pltpu.VMEM((5, 3, 16, 2048), F32), pltpu.SemaphoreType.DMA((5,))],
        compiler_params=params(),
        name="unpack",
    )(final)
    energy = energy + other_energy
    return swapped, energy[:5, :16]


def solution(mesh):
    placed = (
        P("rep", None, "tm", "space"),
        P("space"),
        P("space"),
        P("rep"),
        P("rep"),
        P(None, "rep", "tm", "space"),
        P("rep"),
        P("rep"),
    )
    return jax.shard_map(
        on_device,
        mesh=mesh,
        in_specs=placed,
        out_specs=(P("rep", None, "tm", "space"), P("rep", "tm")),
        check_vma=False,
    )
```
